512 devices in a mesh: step: 64 (over x, z), tp: 8 (over y, core).
Axes of the slice: x: 4, y: 4, z: 16, core: 2. Of those that a mesh axis runs over, the one named last changes fastest.
Arguments:
- trajectory: float32 [64, 128, 5120], P('step', None, 'tp'), may hold values from -3 to 3
- timesteps: int32 [64], replicated, may hold values from 1 to 999, as said below
- context_keys: bfloat16 [512, 3072], P(None, 'tp'), may hold values from -200 to 200
- context_values: bfloat16 [512, 3072], P(None, 'tp'), may hold values from -6 to 6
- ln_gain: float32 [5120], P('tp'), may hold values from 0.1 to 1.9
- q_gain: float32 [3072], P('tp'), may hold values from 0.1 to 1.9
- w_query: bfloat16 [5120, 3072], P('step', 'tp'), may hold values from -0.078125 to 0.078125
- w_out: bfloat16 [3072, 5120], P('step', 'tp'), may hold values from -0.625 to 0.625
Outputs:
- new_trajectory: float32 [64, 128, 5120], P('step', None, 'tp')
- errors: float32 [64], P('step')
The draws below stay inside these ranges and needn't reach their ends.
Inputs may be any that keep to these rules, and one draw needn't show every extreme that they name: `timesteps`: strictly decreasing over the steps; the first is 999.
All inputs are finite; a program needn't handle non-finite values.
Results may differ from the reference program's by a relative error of at most 0.002.
The reference program's roundings to bfloat16 on the way count: a program that leaves them out, or rounds other values in their place, can miss the bound.
Values may be sent and summed in bfloat16 or wider, within the bound.
No kernel may reach another device: no remote copies, remote signals or barrier semaphores. Data moves between devices by JAX's collectives and lax.ppermute only.
A program may use at most 64 MiB of HBM per device.

```python
import math
import jax
import jax.numpy as jnp
from jax import lax

D = 5120
HD = 128
HEADS = 24
TOK = 128
TXT = 512
HC = 3072
STEPS = 64


def draw_trajectory(key, part):
    key = jax.random.fold_in(key, 5)
    common_key, own_key = jax.random.split(key)
    common = 0.3 * jax.random.normal(common_key, (1, TOK, D), jnp.float32)
    own = 0.1 * jax.random.normal(own_key, (STEPS, TOK, D), jnp.float32)
    return jnp.clip(common + own, -3.0, 3.0)


def draw_timesteps(key, part):
    key = jax.random.fold_in(key, 7)
    picks = jax.random.permutation(key, 998)[:STEPS - 1] + 1
    ordered = -jnp.sort(-picks)
    return jnp.concatenate([jnp.array([999], jnp.int32), ordered.astype(jnp.int32)])


def draw_context_keys(key, part):
    key = jax.random.fold_in(key, 11)
    first_key = jax.random.fold_in(key, 0)
    base = jax.random.normal(first_key, (TXT, HC), jnp.float32)
    return jnp.clip(base, -200.0, 200.0).astype(jnp.bfloat16)


def block_levels(stream_key, shape, cuts, least, top_value):
    factor_of, own = 1.0, jax.random.fold_in(stream_key, 6)
    for axis_at, blocks in cuts:
        steps = jnp.exp(jax.random.uniform(jax.random.fold_in(own, axis_at), (blocks,), jnp.float32, least / len(cuts), top_value / len(cuts)))
        factor_of = factor_of * jnp.repeat(steps, shape[axis_at] // blocks).reshape([-1 if axis == axis_at else 1 for axis in range(len(shape))])
    return factor_of


def normal_values(key, extent, scale, most, pieces=(), kind=jnp.bfloat16):
    level = block_levels(key, extent, pieces, -0.22, 0.18) if pieces else 1.0
    values = jax.random.normal(key, extent, jnp.float32) * scale * level
    return jnp.minimum(jnp.maximum(values, -most), most).astype(kind)


def setup_inputs(seed: int = 0) -> dict:
    keys = jax.random.split(jax.random.key(seed), 9)
    trajectory = draw_trajectory(jax.random.fold_in(keys[8], 71), 0)
    timesteps = draw_timesteps(jax.random.fold_in(keys[8], 71), 0)
    context_keys = draw_context_keys(jax.random.fold_in(keys[8], 71), 0)
    context_values = normal_values(keys[3], (TXT, HC), 1.0, 6.0, ((1, 8),))
    ln_gain = jnp.clip(1.0 + 0.18 * jax.random.normal(keys[4], (D,), jnp.float32), 0.1, 1.9)
    q_gain = jnp.clip(1.0 + 0.18 * jax.random.normal(keys[5], (HC,), jnp.float32), 0.1, 1.9)
    w_query = normal_values(keys[6], (D, HC), D ** -0.5, 0.078125, ((0, 64), (1, 8)))
    w_out = normal_values(keys[7], (HC, D), (HC // 32) ** -0.5, 0.625, ((0, 64), (1, 8)))
    return {"trajectory": trajectory, "timesteps": timesteps, "context_keys": context_keys, "context_values": context_values, "ln_gain": ln_gain, "q_gain": q_gain, "w_query": w_query, "w_out": w_out}


epsilon = 1e-06

def sigma_of(levels):
    scaled = levels.astype(jnp.float32) / 1000.0
    return 5.0 * scaled / (1.0 + 4.0 * scaled)

def layer_norm(values_in, gains):
    row_mean = lax.optimization_barrier(jnp.mean(values_in, axis=-1, keepdims=True))
    row_square = lax.optimization_barrier(jnp.mean(values_in * values_in, axis=-1, keepdims=True))
    row_var = row_square - row_mean * row_mean
    return ((values_in - row_mean) * lax.rsqrt(row_var + epsilon) * gains).astype(jnp.bfloat16)

def reference(trajectory, timesteps, context_keys, context_values, ln_gain, q_gain, w_query, w_out):
    later = jnp.concatenate([timesteps[1:], jnp.zeros((1,), jnp.int32)])
    step_sizes = sigma_of(later) - sigma_of(timesteps)
    key_heads = context_keys.astype(jnp.float32).reshape(TXT, HEADS, HD)
    value_heads = context_values.astype(jnp.float32).reshape(TXT, HEADS, HD)

    def one_step(packed):
        state, step_size = packed
        normed = layer_norm(state, ln_gain)
        query = jnp.dot(normed, w_query, preferred_element_type=jnp.float32)
        query_scale = lax.rsqrt(lax.optimization_barrier(jnp.mean(query * query, axis=-1, keepdims=True)) + epsilon)
        q_normed = (query * query_scale * q_gain).astype(jnp.bfloat16)
        q_heads = q_normed.astype(jnp.float32).reshape(TOK, HEADS, HD)
        scores = jnp.einsum('thd,khd->htk', q_heads, key_heads) / math.sqrt(HD)
        soft_weights = jax.nn.softmax(scores, axis=-1).astype(jnp.bfloat16)
        attended = jnp.einsum('htk,khd->thd', soft_weights.astype(jnp.float32), value_heads)
        attended = attended.reshape(TOK, HC).astype(jnp.bfloat16)
        velocity = jnp.dot(attended, w_out, preferred_element_type=jnp.float32)
        return step_size * velocity
    drift = lax.map(one_step, (trajectory, step_sizes))
    running = jnp.cumsum(drift, axis=0)
    earlier = jnp.concatenate([jnp.zeros_like(drift[:1]), running[:-1]], axis=0)
    before = trajectory[0][None] + earlier
    new_trajectory = before + drift
    change = before - trajectory
    errors = lax.optimization_barrier(jnp.mean(change * change, axis=(1, 2)))
    return (new_trajectory, errors)
```

```python
import math

import jax
import jax.numpy as jnp
from jax import lax
from jax.sharding import Mesh
from jax.sharding import PartitionSpec as P

HD = 128
STEP = ("x", "z")
TP = ("y", "core")

epsilon = 1e-06


def sigma_of(levels):
    scaled = levels.astype(jnp.float32) / 1000.0
    return 5.0 * scaled / (1.0 + 4.0 * scaled)


def transpose_plane(value):
    side = lax.axis_size("x")
    pairs = [(a * side + b, b * side + a) for a in range(side) for b in range(side)]
    return lax.ppermute(value, ("x", "y"), pairs)


def prefix_over_steps(term):
    z_size, x_size = lax.axis_size("z"), lax.axis_size("x")
    rows, width = term.shape
    slices = lax.all_to_all(term.reshape(z_size, rows // z_size, width), "z", 0, 0)
    running = [slices[0]]
    for at in range(1, z_size):
        running.append(running[-1] + slices[at])
    totals = lax.all_gather(running[-1], "x")
    mine = lax.axis_index("x")
    earlier = jnp.zeros_like(running[0])
    for at in range(x_size - 1):
        earlier = earlier + jnp.where(at < mine, totals[at], 0.0)
    summed = jnp.stack(running) + earlier[None]
    return lax.all_to_all(summed, "z", 0, 0).reshape(rows, width)


def on_device(trajectory, timesteps, context_keys, context_values, ln_gain, q_gain, w_query, w_out):
    latent = trajectory[0]
    token_count, block = latent.shape
    full_width = block * lax.axis_size(TP)
    x_size = lax.axis_size("x")

    query_rows = lax.all_gather(w_query, "z", axis=0, tiled=True)
    out_rows = lax.all_gather(w_out, "x")
    out_rows = lax.all_gather(out_rows, "z", axis=1)
    out_rows = out_rows.reshape(-1, w_out.shape[1])

    sums = jnp.stack([jnp.sum(latent, axis=-1), jnp.sum(latent * latent, axis=-1)])
    sums = lax.psum(sums, TP) / full_width
    row_mean, row_square = sums[0][:, None], sums[1][:, None]
    row_var = row_square - row_mean * row_mean
    normed = ((latent - row_mean) * lax.rsqrt(row_var + epsilon) * ln_gain).astype(jnp.bfloat16)

    flipped = transpose_plane(normed)
    half = token_count // 2
    parts = [lax.all_gather(flipped[at * half : (at + 1) * half], TP) for at in range(2)]
    query_weights = query_rows.reshape(2, block, -1)
    partial = []
    for part in parts:
        part = part.reshape(x_size, 2, half, block)
        partial.append(
            jnp.einsum("xctk,ckn->xtn", part, query_weights, preferred_element_type=jnp.float32)
        )
    partial = jnp.concatenate(partial, axis=1)
    query = jnp.sum(lax.all_to_all(partial, "x", 0, 0), axis=0)

    query_width = query.shape[1] * lax.axis_size(TP)
    square_sum = lax.psum(jnp.sum(query * query, axis=-1), TP)
    query_scale = lax.rsqrt(square_sum / query_width + epsilon)[:, None]
    q_normed = (query * query_scale * q_gain).astype(jnp.bfloat16)
    local_heads = query.shape[1] // HD
    q_heads = q_normed.reshape(token_count, local_heads, HD)
    key_heads = context_keys.reshape(context_keys.shape[0], local_heads, HD)
    value_heads = context_values.reshape(context_values.shape[0], local_heads, HD)
    scores = jnp.einsum(
        "thd,khd->htk", q_heads, key_heads, preferred_element_type=jnp.float32
    ) / math.sqrt(HD)
    soft_weights = jax.nn.softmax(scores, axis=-1).astype(jnp.bfloat16)
    attended = jnp.einsum(
        "htk,khd->thd", soft_weights, value_heads, preferred_element_type=jnp.float32
    )
    attended = attended.reshape(token_count, local_heads * HD).astype(jnp.bfloat16)
    attended_all = lax.all_gather(attended, TP, axis=1, tiled=True)
    velocity = jnp.dot(attended_all, out_rows, preferred_element_type=jnp.float32)

    position = lax.axis_index(STEP)
    step_total = timesteps.shape[0]
    level_now = timesteps[position]
    level_next = jnp.where(
        position + 1 < step_total, timesteps[jnp.minimum(position + 1, step_total - 1)], 0
    )
    step_size = sigma_of(level_next) - sigma_of(level_now)
    drift = step_size * velocity
    first = position == 0
    new_rows = prefix_over_steps(drift + jnp.where(first, latent, 0.0))
    before = jnp.where(first, latent, new_rows - drift)
    change = before - latent
    change_sum = lax.psum(jnp.sum(change * change), TP)
    error_value = change_sum / (token_count * full_width)
    return (new_rows[None], error_value.reshape(1))


def solution(mesh):
    fine = Mesh(mesh.devices.reshape(4, 16, 4, 2), ("x", "z", "y", "core"))
    placed = (
        P(STEP, None, TP),
        P(),
        P(None, TP),
        P(None, TP),
        P(TP),
        P(TP),
        P(STEP, TP),
        P(STEP, TP),
    )
    return jax.shard_map(
        on_device,
        mesh=fine,
        in_specs=placed,
        out_specs=(P(STEP, None, TP), P(STEP)),
        check_vma=False,
    )
```

```python
import math

import jax
import jax.numpy as jnp
from jax import lax
from jax.sharding import Mesh
from jax.sharding import PartitionSpec as P

HD = 128
STEP = ("x", "z")
TP = ("y", "core")

epsilon = 1e-06


def sigma_of(levels):
    scaled = levels.astype(jnp.float32) / 1000.0
    return 5.0 * scaled / (1.0 + 4.0 * scaled)


def tp_sum(value):
    return lax.psum(lax.psum(value, "core"), "y")


def transpose_plane(value):
    side = lax.axis_size("x")
    pairs = [(a * side + b, b * side + a) for a in range(side) for b in range(side)]
    return lax.ppermute(value, ("x", "y"), pairs)


def prefix_over_steps(term):
    z_size, x_size = lax.axis_size("z"), lax.axis_size("x")
    rows, width = term.shape
    slices = lax.all_to_all(term.reshape(z_size, rows // z_size, width), "z", 0, 0)
    running = [slices[0]]
    for at in range(1, z_size):
        running.append(running[-1] + slices[at])
    totals = lax.all_gather(running[-1], "x")
    mine = lax.axis_index("x")
    earlier = jnp.zeros_like(running[0])
    for at in range(x_size - 1):
        earlier = earlier + jnp.where(at < mine, totals[at], 0.0)
    summed = jnp.stack(running) + earlier[None]
    return lax.all_to_all(summed, "z", 0, 0).reshape(rows, width)


def on_device(trajectory, timesteps, context_keys, context_values, ln_gain, q_gain, w_query, w_out):
    latent = trajectory[0]
    token_count, block = latent.shape
    full_width = block * lax.axis_size(TP)
    x_size = lax.axis_size("x")

    query_depth, query_cols = w_query.shape
    both = jnp.concatenate([jnp.pad(w_query, ((0, 0), (0, block - query_cols))), w_out])
    both = lax.all_gather(both, "z")
    query_rows = both[:, :query_depth, :query_cols].reshape(-1, query_cols)
    out_rows = both[:, query_depth:].reshape(-1, block)
    out_rows = lax.all_gather(out_rows, "x", axis=0, tiled=True)

    sums = jnp.stack([jnp.sum(latent, axis=-1), jnp.sum(latent * latent, axis=-1)])
    sums = tp_sum(sums) / full_width
    row_mean, row_square = sums[0][:, None], sums[1][:, None]
    row_var = row_square - row_mean * row_mean
    normed = ((latent - row_mean) * lax.rsqrt(row_var + epsilon) * ln_gain).astype(jnp.bfloat16)

    flipped = transpose_plane(normed)
    gathered = lax.all_gather(flipped, "y")
    half = x_size // 2
    query_weights = query_rows.reshape(2, block, query_cols)
    partial = []
    for at in range(2):
        part = lax.all_gather(gathered[at * half : (at + 1) * half], "core")
        partial.append(
            jnp.einsum("cxtk,ckn->xtn", part, query_weights, preferred_element_type=jnp.float32)
        )
    partial = jnp.concatenate(partial)
    query = jnp.sum(lax.all_to_all(partial, "x", 0, 0), axis=0)

    query_width = query.shape[1] * lax.axis_size(TP)
    square_sum = tp_sum(jnp.sum(query * query, axis=-1))
    query_scale = lax.rsqrt(square_sum / query_width + epsilon)[:, None]
    q_normed = (query * query_scale * q_gain).astype(jnp.bfloat16)
    local_heads = query.shape[1] // HD
    q_heads = q_normed.reshape(token_count, local_heads, HD)
    key_heads = context_keys.reshape(context_keys.shape[0], local_heads, HD)
    value_heads = context_values.reshape(context_values.shape[0], local_heads, HD)
    scores = jnp.einsum(
        "thd,khd->htk", q_heads, key_heads, preferred_element_type=jnp.float32
    ) / math.sqrt(HD)
    soft_weights = jax.nn.softmax(scores, axis=-1).astype(jnp.bfloat16)
    attended = jnp.einsum(
        "htk,khd->thd", soft_weights, value_heads, preferred_element_type=jnp.float32
    )
    attended = attended.reshape(token_count, local_heads * HD).astype(jnp.bfloat16)
    attended_all = lax.all_gather(attended, TP, axis=1, tiled=True)
    velocity = jnp.dot(attended_all, out_rows, preferred_element_type=jnp.float32)

    position = lax.axis_index(STEP)
    step_total = timesteps.shape[0]
    level_now = timesteps[position]
    level_next = jnp.where(
        position + 1 < step_total, timesteps[jnp.minimum(position + 1, step_total - 1)], 0
    )
    step_size = sigma_of(level_next) - sigma_of(level_now)
    drift = step_size * velocity
    first = position == 0
    new_rows = prefix_over_steps(drift + jnp.where(first, latent, 0.0))
    before = jnp.where(first, latent, new_rows - drift)
    change = before - latent
    change_sum = tp_sum(jnp.sum(change * change))
    error_value = change_sum / (token_count * full_width)
    return (new_rows[None], error_value.reshape(1))


def solution(mesh):
    fine = Mesh(mesh.devices.reshape(4, 16, 4, 2), ("x", "z", "y", "core"))
    placed = (
        P(STEP, None, TP),
        P(),
        P(None, TP),
        P(None, TP),
        P(TP),
        P(TP),
        P(STEP, TP),
        P(STEP, TP),
    )
    return jax.shard_map(
        on_device,
        mesh=fine,
        in_specs=placed,
        out_specs=(P(STEP, None, TP), P(STEP)),
        check_vma=False,
    )
```

```python
import math

import jax
import jax.numpy as jnp
from jax import lax
from jax.sharding import Mesh
from jax.sharding import PartitionSpec as P

HD = 128
STEP = ("x", "z")
TP = ("y", "core")

epsilon = 1e-06


def sigma_of(levels):
    scaled = levels.astype(jnp.float32) / 1000.0
    return 5.0 * scaled / (1.0 + 4.0 * scaled)


def tp_sum(value):
    return lax.psum(lax.psum(value, "core"), "y")


def transpose_plane(value):
    side = lax.axis_size("x")
    pairs = [(a * side + b, b * side + a) for a in range(side) for b in range(side)]
    return lax.ppermute(value, ("x", "y"), pairs)


def prefix_over_steps(term):
    z_size, x_size = lax.axis_size("z"), lax.axis_size("x")
    rows, width = term.shape
    slices = lax.all_to_all(term.reshape(z_size, rows // z_size, width), "z", 0, 0)
    running = [slices[0]]
    for at in range(1, z_size):
        running.append(running[-1] + slices[at])
    totals = lax.all_gather(running[-1], "x")
    mine = lax.axis_index("x")
    earlier = jnp.zeros_like(running[0])
    for at in range(x_size - 1):
        earlier = earlier + jnp.where(at < mine, totals[at], 0.0)
    summed = jnp.stack(running) + earlier[None]
    return lax.all_to_all(summed, "z", 0, 0).reshape(rows, width)


def on_device(trajectory, timesteps, context_keys, context_values, ln_gain, q_gain, w_query, w_out):
    latent = trajectory[0]
    token_count, block = latent.shape
    full_width = block * lax.axis_size(TP)
    x_size = lax.axis_size("x")

    query_depth, query_cols = w_query.shape
    both = jnp.concatenate([jnp.pad(w_query, ((0, 0), (0, block - query_cols))), w_out])
    both = lax.all_gather(both, "z")

    sums = jnp.stack([jnp.sum(latent, axis=-1), jnp.sum(latent * latent, axis=-1)])
    sums = tp_sum(sums) / full_width
    row_mean, row_square = sums[0][:, None], sums[1][:, None]
    row_var = row_square - row_mean * row_mean
    normed = ((latent - row_mean) * lax.rsqrt(row_var + epsilon) * ln_gain).astype(jnp.bfloat16)

    flipped = transpose_plane(normed)
    gathered = lax.all_gather(flipped, "y")
    half = x_size // 2
    parts = [lax.all_gather(gathered[at * half : (at + 1) * half], "core") for at in range(2)]
    both, parts = lax.optimization_barrier((both, parts))
    query_weights = both[:, :query_depth, :query_cols].reshape(2, block, query_cols)
    out_rows = both[:, query_depth:].reshape(-1, block)
    out_rows = lax.all_gather(out_rows, "x", axis=0, tiled=True)
    partial = [
        jnp.einsum("cxtk,ckn->xtn", part, query_weights, preferred_element_type=jnp.float32)
        for part in parts
    ]
    partial = jnp.concatenate(partial)
    query = jnp.sum(lax.all_to_all(partial, "x", 0, 0), axis=0)

    query_width = query.shape[1] * lax.axis_size(TP)
    square_sum = tp_sum(jnp.sum(query * query, axis=-1))
    query_scale = lax.rsqrt(square_sum / query_width + epsilon)[:, None]
    q_normed = (query * query_scale * q_gain).astype(jnp.bfloat16)
    local_heads = query.shape[1] // HD
    q_heads = q_normed.reshape(token_count, local_heads, HD)
    key_heads = context_keys.reshape(context_keys.shape[0], local_heads, HD)
    value_heads = context_values.reshape(context_values.shape[0], local_heads, HD)
    scores = jnp.einsum(
        "thd,khd->htk", q_heads, key_heads, preferred_element_type=jnp.float32
    ) / math.sqrt(HD)
    soft_weights = jax.nn.softmax(scores, axis=-1).astype(jnp.bfloat16)
    attended = jnp.einsum(
        "htk,khd->thd", soft_weights, value_heads, preferred_element_type=jnp.float32
    )
    attended = attended.reshape(token_count, local_heads * HD).astype(jnp.bfloat16)
    attended_all = lax.all_gather(attended, TP, axis=1, tiled=True)
    velocity = jnp.dot(attended_all, out_rows, preferred_element_type=jnp.float32)

    position = lax.axis_index(STEP)
    step_total = timesteps.shape[0]
    level_now = timesteps[position]
    level_next = jnp.where(
        position + 1 < step_total, timesteps[jnp.minimum(position + 1, step_total - 1)], 0
    )
    step_size = sigma_of(level_next) - sigma_of(level_now)
    drift = step_size * velocity
    first = position == 0
    new_rows = prefix_over_steps(drift + jnp.where(first, latent, 0.0))
    before = jnp.where(first, latent, new_rows - drift)
    change = before - latent
    change_sum = tp_sum(jnp.sum(change * change))
    error_value = change_sum / (token_count * full_width)
    return (new_rows[None], error_value.reshape(1))


def solution(mesh):
    fine = Mesh(mesh.devices.reshape(4, 16, 4, 2), ("x", "z", "y", "core"))
    placed = (
        P(STEP, None, TP),
        P(),
        P(None, TP),
        P(None, TP),
        P(TP),
        P(TP),
        P(STEP, TP),
        P(STEP, TP),
    )
    return jax.shard_map(
        on_device,
        mesh=fine,
        in_specs=placed,
        out_specs=(P(STEP, None, TP), P(STEP)),
        check_vma=False,
    )
```

```python
import math

import jax
import jax.numpy as jnp
from jax import lax
from jax.sharding import Mesh
from jax.sharding import PartitionSpec as P

HD = 128
STEP = ("x", "z")
TP = ("y", "core")

epsilon = 1e-06


def sigma_of(levels):
    scaled = levels.astype(jnp.float32) / 1000.0
    return 5.0 * scaled / (1.0 + 4.0 * scaled)


def tp_sum(value):
    return lax.psum(lax.psum(value, "core"), "y")


def transpose_plane(value):
    side = lax.axis_size("x")
    pairs = [(a * side + b, b * side + a) for a in range(side) for b in range(side)]
    return lax.ppermute(value, ("x", "y"), pairs)


def on_device(trajectory, timesteps, context_keys, context_values, ln_gain, q_gain, w_query, w_out):
    latent = trajectory[0]
    token_count, block = latent.shape
    full_width = block * lax.axis_size(TP)
    x_size = lax.axis_size("x")

    z_size = lax.axis_size("z")
    x_here = lax.axis_index("x")
    slice_tokens = token_count // z_size

    rows_here = lax.all_to_all(latent.reshape(z_size, slice_tokens, block), "z", 0, 0)

    out_depth = w_out.shape[0]
    out_rows = lax.all_gather(jnp.pad(w_out, ((0, 16), (0, 0))), "z")

    sums = jnp.stack([jnp.sum(latent, axis=-1), jnp.sum(latent * latent, axis=-1)])
    sums = tp_sum(sums) / full_width
    row_mean, row_square = sums[0][:, None], sums[1][:, None]
    row_var = row_square - row_mean * row_mean
    normed = ((latent - row_mean) * lax.rsqrt(row_var + epsilon) * ln_gain).astype(jnp.bfloat16)

    w_query, normed = lax.optimization_barrier((w_query, normed))
    query_rows = lax.all_gather(w_query, "z")
    flipped = transpose_plane(normed)
    gathered = lax.all_gather(flipped, "y")
    half = x_size // 2
    parts = [lax.all_gather(gathered[at * half : (at + 1) * half], "core") for at in range(2)]
    query_weights = query_rows.reshape(2, block, w_query.shape[1])
    partial = [
        jnp.einsum("cxtk,ckn->xtn", part, query_weights, preferred_element_type=jnp.float32)
        for part in parts
    ]
    partial = jnp.concatenate(partial)
    out_rows, partial = lax.optimization_barrier((out_rows, partial))
    out_rows = out_rows[:, :out_depth].reshape(-1, block)
    out_rows = lax.all_gather(out_rows, "x", axis=0, tiled=True)
    query = jnp.sum(lax.all_to_all(partial, "x", 0, 0), axis=0)

    query_width = query.shape[1] * lax.axis_size(TP)
    square_sum = tp_sum(jnp.sum(query * query, axis=-1))
    query_scale = lax.rsqrt(square_sum / query_width + epsilon)[:, None]
    q_normed = (query * query_scale * q_gain).astype(jnp.bfloat16)
    local_heads = query.shape[1] // HD
    q_heads = q_normed.reshape(token_count, local_heads, HD)
    key_heads = context_keys.reshape(context_keys.shape[0], local_heads, HD)
    value_heads = context_values.reshape(context_values.shape[0], local_heads, HD)
    scores = jnp.einsum(
        "thd,khd->htk", q_heads, key_heads, preferred_element_type=jnp.float32
    ) / math.sqrt(HD)
    soft_weights = jax.nn.softmax(scores, axis=-1).astype(jnp.bfloat16)
    attended = jnp.einsum(
        "htk,khd->thd", soft_weights, value_heads, preferred_element_type=jnp.float32
    )
    attended = attended.reshape(token_count, local_heads * HD).astype(jnp.bfloat16)
    attended = attended.reshape(z_size, slice_tokens, -1)
    attended = lax.all_to_all(attended, "z", 0, 0).reshape(token_count, -1)
    attended_all = lax.all_gather(attended, TP, axis=1, tiled=True)
    velocity = jnp.dot(attended_all, out_rows, preferred_element_type=jnp.float32)
    velocity = velocity.reshape(z_size, slice_tokens, block)

    later = jnp.concatenate([timesteps[1:], jnp.zeros((1,), timesteps.dtype)])
    step_sizes = sigma_of(later) - sigma_of(timesteps)
    step_sizes = lax.dynamic_slice_in_dim(step_sizes, x_here * z_size, z_size)
    drift = step_sizes[:, None, None] * velocity

    running = [drift[0]]
    for at in range(1, z_size):
        running.append(running[-1] + drift[at])
    start = jnp.where(x_here == 0, rows_here[0], 0.0)
    totals = lax.all_gather(running[-1] + start, "x")
    for at in range(x_size - 1):
        start = start + jnp.where(at < x_here, totals[at], 0.0)
    ends = jnp.stack([start] + [start + one for one in running])
    new_rows = lax.all_to_all(ends[1:], "z", 0, 0).reshape(token_count, block)

    change = ends[:-1] - rows_here
    change_sum = jnp.sum(change * change, axis=(1, 2))
    change_sum = tp_sum(jnp.broadcast_to(change_sum[:, None, None], (z_size, 1, 128)))
    change_sum = jnp.sum(lax.all_to_all(change_sum, "z", 0, 0)[:, 0, 0])
    error_value = change_sum / (token_count * full_width)
    return (new_rows[None], error_value.reshape(1))


def solution(mesh):
    fine = Mesh(mesh.devices.reshape(4, 16, 4, 2), ("x", "z", "y", "core"))
    placed = (
        P(STEP, None, TP),
        P(),
        P(None, TP),
        P(None, TP),
        P(TP),
        P(TP),
        P(STEP, TP),
        P(STEP, TP),
    )
    return jax.shard_map(
        on_device,
        mesh=fine,
        in_specs=placed,
        out_specs=(P(STEP, None, TP), P(STEP)),
        check_vma=False,
    )
```

```python
import math

import jax
import jax.numpy as jnp
from jax import lax
from jax.sharding import Mesh
from jax.sharding import PartitionSpec as P

HD = 128
STEP = ("x", "z")
TP = ("y", "core")

epsilon = 1e-06


def sigma_of(levels):
    scaled = levels.astype(jnp.float32) / 1000.0
    return 5.0 * scaled / (1.0 + 4.0 * scaled)


def tp_sum(value):
    return lax.psum(lax.psum(value, "core"), "y")


def transpose_plane(value):
    side = lax.axis_size("x")
    pairs = [(a * side + b, b * side + a) for a in range(side) for b in range(side)]
    return lax.ppermute(value, ("x", "y"), pairs)


def on_device(trajectory, timesteps, context_keys, context_values, ln_gain, q_gain, w_query, w_out):
    latent = trajectory[0]
    token_count, block = latent.shape
    full_width = block * lax.axis_size(TP)
    x_size = lax.axis_size("x")

    z_size = lax.axis_size("z")
    x_here = lax.axis_index("x")
    slice_tokens = token_count // z_size

    rows_here = lax.all_to_all(latent.reshape(z_size, slice_tokens, block), "z", 0, 0)

    depth, cols = w_query.shape
    query_rows = lax.all_to_all(jnp.broadcast_to(w_query, (z_size, depth, cols)), "z", 0, 0)

    out_depth = w_out.shape[0]
    out_rows = lax.all_gather(jnp.pad(w_out, ((0, 16), (0, 0))), "z")

    sums = jnp.stack([jnp.sum(latent, axis=-1), jnp.sum(latent * latent, axis=-1)])
    sums = tp_sum(sums) / full_width
    row_mean, row_square = sums[0][:, None], sums[1][:, None]
    row_var = row_square - row_mean * row_mean
    normed = ((latent - row_mean) * lax.rsqrt(row_var + epsilon) * ln_gain).astype(jnp.bfloat16)

    flipped = transpose_plane(normed)
    gathered = lax.all_gather(flipped, "y")
    half = x_size // 2
    parts = [lax.all_gather(gathered[at * half : (at + 1) * half], "core") for at in range(2)]
    query_weights = query_rows.reshape(2, block, cols)
    partial = [
        jnp.einsum("cxtk,ckn->xtn", part, query_weights, preferred_element_type=jnp.float32)
        for part in parts
    ]
    partial = jnp.concatenate(partial)
    query = jnp.sum(lax.all_to_all(partial, "x", 0, 0), axis=0)
    out_rows, query = lax.optimization_barrier((out_rows, query))
    out_rows = out_rows[:, :out_depth].reshape(-1, block)
    out_rows = lax.all_gather(out_rows, "x", axis=0, tiled=True)

    query_width = query.shape[1] * lax.axis_size(TP)
    square_sum = tp_sum(jnp.sum(query * query, axis=-1))
    query_scale = lax.rsqrt(square_sum / query_width + epsilon)[:, None]
    q_normed = (query * query_scale * q_gain).astype(jnp.bfloat16)
    local_heads = query.shape[1] // HD
    q_heads = q_normed.reshape(token_count, local_heads, HD)
    key_heads = context_keys.reshape(context_keys.shape[0], local_heads, HD)
    value_heads = context_values.reshape(context_values.shape[0], local_heads, HD)
    scores = jnp.einsum(
        "thd,khd->htk", q_heads, key_heads, preferred_element_type=jnp.float32
    ) / math.sqrt(HD)
    soft_weights = jax.nn.softmax(scores, axis=-1).astype(jnp.bfloat16)
    attended = jnp.einsum(
        "htk,khd->thd", soft_weights, value_heads, preferred_element_type=jnp.float32
    )
    attended = attended.reshape(token_count, local_heads * HD).astype(jnp.bfloat16)
    attended = attended.reshape(z_size, slice_tokens, -1)
    attended = lax.all_to_all(attended, "z", 0, 0).reshape(token_count, -1)
    attended_all = lax.all_gather(attended, TP, axis=1, tiled=True)
    velocity = jnp.dot(attended_all, out_rows, preferred_element_type=jnp.float32)
    velocity = velocity.reshape(z_size, slice_tokens, block)

    later = jnp.concatenate([timesteps[1:], jnp.zeros((1,), timesteps.dtype)])
    step_sizes = sigma_of(later) - sigma_of(timesteps)
    step_sizes = lax.dynamic_slice_in_dim(step_sizes, x_here * z_size, z_size)
    drift = step_sizes[:, None, None] * velocity

    running = drift
    reach = 1
    while reach < z_size:
        running = running + jnp.pad(running[:-reach], ((reach, 0), (0, 0), (0, 0)))
        reach *= 2
    start = jnp.where(x_here == 0, rows_here[0], 0.0)
    totals = lax.all_gather(running[-1] + start, "x")
    for at in range(x_size - 1):
        start = start + jnp.where(at < x_here, totals[at], 0.0)
    change = start + jnp.pad(running[:-1], ((1, 0), (0, 0), (0, 0))) - rows_here
    change_sum = jnp.sum(change * change, axis=(1, 2), keepdims=True)
    change_sum = jnp.broadcast_to(change_sum, (z_size, slice_tokens, HD))
    sent = jnp.concatenate([start + running, change_sum], axis=2)
    got = lax.all_to_all(sent, "z", 0, 0)
    new_rows = got[:, :, :block].reshape(token_count, block)
    change_sum = tp_sum(jnp.sum(got[:, 0, block]))
    error_value = change_sum / (token_count * full_width)
    return (new_rows[None], error_value.reshape(1))


def solution(mesh):
    fine = Mesh(mesh.devices.reshape(4, 16, 4, 2), ("x", "z", "y", "core"))
    placed = (
        P(STEP, None, TP),
        P(),
        P(None, TP),
        P(None, TP),
        P(TP),
        P(TP),
        P(STEP, TP),
        P(STEP, TP),
    )
    return jax.shard_map(
        on_device,
        mesh=fine,
        in_specs=placed,
        out_specs=(P(STEP, None, TP), P(STEP)),
        check_vma=False,
    )
```

```python
import math

import jax
import jax.numpy as jnp
from jax import lax
from jax.sharding import Mesh
from jax.sharding import PartitionSpec as P

HD = 128
STEP = ("x", "z")
TP = ("y", "core")

epsilon = 1e-06


def sigma_of(levels):
    scaled = levels.astype(jnp.float32) / 1000.0
    return 5.0 * scaled / (1.0 + 4.0 * scaled)


def tp_sum(value):
    return lax.psum(lax.psum(value, "core"), "y")


def transpose_plane(value):
    side = lax.axis_size("x")
    pairs = [(a * side + b, b * side + a) for a in range(side) for b in range(side)]
    return lax.ppermute(value, ("x", "y"), pairs)


def gather_by_permutes(value, axis):
    size, mine = lax.axis_size(axis), lax.axis_index(axis)
    whole = jnp.broadcast_to(value, (size, *value.shape))
    for shift in range(1, size):
        pairs = [(at, (at + shift) % size) for at in range(size)]
        got = lax.ppermute(value, axis, pairs)
        whole = lax.dynamic_update_index_in_dim(whole, got, (mine - shift) % size, 0)
    return whole


def on_device(trajectory, timesteps, context_keys, context_values, ln_gain, q_gain, w_query, w_out):
    latent = trajectory[0]
    token_count, block = latent.shape
    full_width = block * lax.axis_size(TP)
    x_size = lax.axis_size("x")

    z_size = lax.axis_size("z")
    x_here = lax.axis_index("x")
    slice_tokens = token_count // z_size

    rows_here = lax.all_to_all(latent.reshape(z_size, slice_tokens, block), "z", 0, 0)

    moved, moved_gain = transpose_plane(latent), transpose_plane(ln_gain)

    out_rows = gather_by_permutes(w_out, "x")

    depth, cols = w_query.shape
    query_rows = lax.all_to_all(jnp.broadcast_to(w_query, (z_size, depth, cols)), "z", 0, 0)

    sums = jnp.stack([jnp.sum(moved, axis=-1), jnp.sum(moved * moved, axis=-1)])
    sums = lax.psum(lax.psum(sums, "core"), "x") / full_width
    row_mean, row_square = sums[0][:, None], sums[1][:, None]
    row_var = row_square - row_mean * row_mean
    normed = ((moved - row_mean) * lax.rsqrt(row_var + epsilon) * moved_gain).astype(jnp.bfloat16)

    gathered = lax.all_gather(normed, "y")
    half = x_size // 2
    parts = [lax.all_gather(gathered[at * half : (at + 1) * half], "core") for at in range(2)]
    out_rows, query_rows, parts = lax.optimization_barrier((out_rows, query_rows, parts))
    out_rows = lax.all_gather(out_rows, "z", axis=1).reshape(-1, block)
    query_weights = query_rows.reshape(2, block, cols)
    partial = [
        jnp.einsum("cxtk,ckn->xtn", part, query_weights, preferred_element_type=jnp.float32)
        for part in parts
    ]
    partial = jnp.concatenate(partial)
    query = jnp.sum(lax.all_to_all(partial, "x", 0, 0), axis=0)
    query_width = query.shape[1] * lax.axis_size(TP)
    square_sum = tp_sum(jnp.sum(query * query, axis=-1))
    query_scale = lax.rsqrt(square_sum / query_width + epsilon)[:, None]
    q_normed = (query * query_scale * q_gain).astype(jnp.bfloat16)
    local_heads = query.shape[1] // HD
    q_heads = q_normed.reshape(token_count, local_heads, HD)
    key_heads = context_keys.reshape(context_keys.shape[0], local_heads, HD)
    value_heads = context_values.reshape(context_values.shape[0], local_heads, HD)
    scores = jnp.einsum(
        "thd,khd->htk", q_heads, key_heads, preferred_element_type=jnp.float32
    ) / math.sqrt(HD)
    soft_weights = jax.nn.softmax(scores, axis=-1).astype(jnp.bfloat16)
    attended = jnp.einsum(
        "htk,khd->thd", soft_weights, value_heads, preferred_element_type=jnp.float32
    )
    attended = attended.reshape(token_count, local_heads * HD).astype(jnp.bfloat16)
    attended = attended.reshape(z_size, slice_tokens, -1)
    attended = lax.all_to_all(attended, "z", 0, 0).reshape(token_count, -1)
    attended_all = lax.all_gather(attended, TP, axis=1, tiled=True)
    velocity = jnp.dot(attended_all, out_rows, preferred_element_type=jnp.float32)
    velocity = velocity.reshape(z_size, slice_tokens, block)

    later = jnp.concatenate([timesteps[1:], jnp.zeros((1,), timesteps.dtype)])
    step_sizes = sigma_of(later) - sigma_of(timesteps)
    step_sizes = lax.dynamic_slice_in_dim(step_sizes, x_here * z_size, z_size)
    drift = step_sizes[:, None, None] * velocity

    running = drift
    reach = 1
    while reach < z_size:
        running = running + jnp.pad(running[:-reach], ((reach, 0), (0, 0), (0, 0)))
        reach *= 2
    start = jnp.where(x_here == 0, rows_here[0], 0.0)
    totals = lax.all_gather(running[-1] + start, "x")
    for at in range(x_size - 1):
        start = start + jnp.where(at < x_here, totals[at], 0.0)
    change = start + jnp.pad(running[:-1], ((1, 0), (0, 0), (0, 0))) - rows_here
    change_sum = tp_sum(lax.psum(jnp.sum(change * change, axis=(1, 2)), "z"))
    change_sum = change_sum[lax.axis_index("z")]
    new_rows = lax.all_to_all(start + running, "z", 0, 0).reshape(token_count, block)
    error_value = change_sum / (token_count * full_width)
    return (new_rows[None], error_value.reshape(1))


def solution(mesh):
    fine = Mesh(mesh.devices.reshape(4, 16, 4, 2), ("x", "z", "y", "core"))
    placed = (
        P(STEP, None, TP),
        P(),
        P(None, TP),
        P(None, TP),
        P(TP),
        P(TP),
        P(STEP, TP),
        P(STEP, TP),
    )
    return jax.shard_map(
        on_device,
        mesh=fine,
        in_specs=placed,
        out_specs=(P(STEP, None, TP), P(STEP)),
        check_vma=False,
    )
```

```python
import math

import jax
import jax.numpy as jnp
from jax import lax
from jax.sharding import Mesh
from jax.sharding import PartitionSpec as P

HD = 128
STEP = ("x", "z")
TP = ("y", "core")

epsilon = 1e-06


def sigma_of(levels):
    scaled = levels.astype(jnp.float32) / 1000.0
    return 5.0 * scaled / (1.0 + 4.0 * scaled)


def tp_sum(value):
    return lax.psum(lax.psum(value, "core"), "y")


def transpose_plane(value):
    side = lax.axis_size("x")
    pairs = [(a * side + b, b * side + a) for a in range(side) for b in range(side)]
    return lax.ppermute(value, ("x", "y"), pairs)


def on_device(trajectory, timesteps, context_keys, context_values, ln_gain, q_gain, w_query, w_out):
    latent = trajectory[0]
    token_count, block = latent.shape
    full_width = block * lax.axis_size(TP)
    x_size = lax.axis_size("x")

    z_size = lax.axis_size("z")
    x_here = lax.axis_index("x")
    slice_tokens = token_count // z_size

    rows_here = lax.all_to_all(latent.reshape(z_size, slice_tokens, block), "z", 0, 0)

    out_rows = lax.all_to_all(jnp.broadcast_to(w_out, (x_size, *w_out.shape)), "x", 0, 0)

    sums = jnp.stack([jnp.sum(latent, axis=-1), jnp.sum(latent * latent, axis=-1)])
    sums = tp_sum(sums) / full_width
    row_mean, row_square = sums[0][:, None], sums[1][:, None]
    row_var = row_square - row_mean * row_mean
    normed = ((latent - row_mean) * lax.rsqrt(row_var + epsilon) * ln_gain).astype(jnp.bfloat16)

    w_query, normed = lax.optimization_barrier((w_query, normed))
    query_rows = lax.all_gather(w_query, "z")
    flipped = transpose_plane(normed)
    out_rows, query_rows, flipped = lax.optimization_barrier((out_rows, query_rows, flipped))
    out_rows = lax.all_gather(out_rows, "z", axis=1).reshape(-1, block)
    gathered = lax.all_gather(flipped, "y")
    half = x_size // 2
    parts = [lax.all_gather(gathered[at * half : (at + 1) * half], "core") for at in range(2)]
    query_weights = query_rows.reshape(2, block, w_query.shape[1])
    partial = [
        jnp.einsum("cxtk,ckn->xtn", part, query_weights, preferred_element_type=jnp.float32)
        for part in parts
    ]
    partial = jnp.concatenate(partial)
    query = jnp.sum(lax.all_to_all(partial, "x", 0, 0), axis=0)
    query_width = query.shape[1] * lax.axis_size(TP)
    square_sum = tp_sum(jnp.sum(query * query, axis=-1))
    query_scale = lax.rsqrt(square_sum / query_width + epsilon)[:, None]
    q_normed = (query * query_scale * q_gain).astype(jnp.bfloat16)
    local_heads = query.shape[1] // HD
    q_heads = q_normed.reshape(token_count, local_heads, HD)
    key_heads = context_keys.reshape(context_keys.shape[0], local_heads, HD)
    value_heads = context_values.reshape(context_values.shape[0], local_heads, HD)
    scores = jnp.einsum(
        "thd,khd->htk", q_heads, key_heads, preferred_element_type=jnp.float32
    ) / math.sqrt(HD)
    soft_weights = jax.nn.softmax(scores, axis=-1).astype(jnp.bfloat16)
    attended = jnp.einsum(
        "htk,khd->thd", soft_weights, value_heads, preferred_element_type=jnp.float32
    )
    attended = attended.reshape(token_count, local_heads * HD).astype(jnp.bfloat16)
    attended = attended.reshape(z_size, slice_tokens, -1)
    attended = lax.all_to_all(attended, "z", 0, 0).reshape(token_count, -1)
    attended_all = lax.all_gather(attended, TP, axis=1, tiled=True)
    velocity = jnp.dot(attended_all, out_rows, preferred_element_type=jnp.float32)
    velocity = velocity.reshape(z_size, slice_tokens, block)

    later = jnp.concatenate([timesteps[1:], jnp.zeros((1,), timesteps.dtype)])
    step_sizes = sigma_of(later) - sigma_of(timesteps)
    step_sizes = lax.dynamic_slice_in_dim(step_sizes, x_here * z_size, z_size)
    drift = step_sizes[:, None, None] * velocity

    running = drift
    reach = 1
    while reach < z_size:
        running = running + jnp.pad(running[:-reach], ((reach, 0), (0, 0), (0, 0)))
        reach *= 2
    start = jnp.where(x_here == 0, rows_here[0], 0.0)
    totals = lax.all_gather(running[-1] + start, "x")
    for at in range(x_size - 1):
        start = start + jnp.where(at < x_here, totals[at], 0.0)
    change = start + jnp.pad(running[:-1], ((1, 0), (0, 0), (0, 0))) - rows_here
    change_sum = tp_sum(jnp.sum(change * change, axis=(1, 2)))
    new_rows = lax.all_to_all(start + running, "z", 0, 0).reshape(token_count, block)
    change_sum, new_rows = lax.optimization_barrier((change_sum, new_rows))
    change_sum = jnp.broadcast_to(change_sum[:, None, None], (z_size, 1, HD))
    change_sum = jnp.sum(lax.all_to_all(change_sum, "z", 0, 0)[:, 0, 0])
    error_value = change_sum / (token_count * full_width)
    return (new_rows[None], error_value.reshape(1))


def solution(mesh):
    fine = Mesh(mesh.devices.reshape(4, 16, 4, 2), ("x", "z", "y", "core"))
    placed = (
        P(STEP, None, TP),
        P(),
        P(None, TP),
        P(None, TP),
        P(TP),
        P(TP),
        P(STEP, TP),
        P(STEP, TP),
    )
    return jax.shard_map(
        on_device,
        mesh=fine,
        in_specs=placed,
        out_specs=(P(STEP, None, TP), P(STEP)),
        check_vma=False,
    )
```

```python
import math

import jax
import jax.numpy as jnp
from jax import lax
from jax.sharding import Mesh
from jax.sharding import PartitionSpec as P

HD = 128
STEP = ("x", "z")
TP = ("y", "core")

epsilon = 1e-06


def sigma_of(levels):
    scaled = levels.astype(jnp.float32) / 1000.0
    return 5.0 * scaled / (1.0 + 4.0 * scaled)


def tp_sum(value):
    return lax.psum(lax.psum(value, "core"), "y")


def transpose_plane(value):
    side = lax.axis_size("x")
    pairs = [(a * side + b, b * side + a) for a in range(side) for b in range(side)]
    return lax.ppermute(value, ("x", "y"), pairs)


def on_device(trajectory, timesteps, context_keys, context_values, ln_gain, q_gain, w_query, w_out):
    latent = trajectory[0]
    token_count, block = latent.shape
    full_width = block * lax.axis_size(TP)
    x_size = lax.axis_size("x")

    z_size = lax.axis_size("z")
    x_here = lax.axis_index("x")
    slice_tokens = token_count // z_size

    rows_here = lax.all_to_all(latent.reshape(z_size, slice_tokens, block), "z", 0, 0)

    depth, cols = w_query.shape
    query_rows = lax.all_to_all(jnp.broadcast_to(w_query, (z_size, depth, cols)), "z", 0, 0)

    out_rows = lax.all_gather(w_out, STEP, axis=0, tiled=True)

    sums = jnp.stack([jnp.sum(latent, axis=-1), jnp.sum(latent * latent, axis=-1)])
    sums = tp_sum(sums) / full_width
    row_mean, row_square = sums[0][:, None], sums[1][:, None]
    row_var = row_square - row_mean * row_mean
    normed = ((latent - row_mean) * lax.rsqrt(row_var + epsilon) * ln_gain).astype(jnp.bfloat16)

    flipped = transpose_plane(normed)
    gathered = lax.all_gather(flipped, "y")
    half = x_size // 2
    parts = [lax.all_gather(gathered[at * half : (at + 1) * half], "core") for at in range(2)]
    query_weights = query_rows.reshape(2, block, cols)
    partial = [
        jnp.einsum("cxtk,ckn->xtn", part, query_weights, preferred_element_type=jnp.float32)
        for part in parts
    ]
    partial = jnp.concatenate(partial)
    query = jnp.sum(lax.all_to_all(partial, "x", 0, 0), axis=0)
    query_width = query.shape[1] * lax.axis_size(TP)
    square_sum = tp_sum(jnp.sum(query * query, axis=-1))
    query_scale = lax.rsqrt(square_sum / query_width + epsilon)[:, None]
    q_normed = (query * query_scale * q_gain).astype(jnp.bfloat16)
    local_heads = query.shape[1] // HD
    q_heads = q_normed.reshape(token_count, local_heads, HD)
    key_heads = context_keys.reshape(context_keys.shape[0], local_heads, HD)
    value_heads = context_values.reshape(context_values.shape[0], local_heads, HD)
    scores = jnp.einsum(
        "thd,khd->htk", q_heads, key_heads, preferred_element_type=jnp.float32
    ) / math.sqrt(HD)
    soft_weights = jax.nn.softmax(scores, axis=-1).astype(jnp.bfloat16)
    attended = jnp.einsum(
        "htk,khd->thd", soft_weights, value_heads, preferred_element_type=jnp.float32
    )
    attended = attended.reshape(token_count, local_heads * HD).astype(jnp.bfloat16)
    attended = attended.reshape(z_size, slice_tokens, -1)
    attended = lax.all_to_all(attended, "z", 0, 0).reshape(token_count, -1)
    later = jnp.concatenate([timesteps[1:], jnp.zeros((1,), timesteps.dtype)])
    step_sizes = sigma_of(later) - sigma_of(timesteps)
    step_sizes = lax.dynamic_slice_in_dim(step_sizes, x_here * z_size, z_size)[:, None, None]

    weighted = jnp.sum(step_sizes * attended.reshape(z_size, slice_tokens, -1), axis=0)
    width = weighted.shape[1]
    sides = lax.all_gather(jnp.concatenate([weighted, rows_here[0]], axis=1), "x")
    weighted = jnp.zeros_like(weighted)
    for at in range(x_size - 1):
        weighted = weighted + jnp.where(at < x_here, sides[at, :, :width], 0.0)
    high = lax.reduce_precision(weighted, 8, 7)
    terms = [high.astype(jnp.bfloat16), (weighted - high).astype(jnp.bfloat16)]
    rows = jnp.concatenate([attended, *terms])

    rows = lax.all_gather(rows, TP, axis=1, tiled=True)
    product = jnp.dot(rows, out_rows, preferred_element_type=jnp.float32)
    velocity = product[:token_count].reshape(z_size, slice_tokens, block)
    terms = product[token_count:].reshape(2, slice_tokens, block)
    start = sides[0, :, width:] + (terms[0] + terms[1])
    drift = step_sizes * velocity

    running = drift
    reach = 1
    while reach < z_size:
        running = running + jnp.pad(running[:-reach], ((reach, 0), (0, 0), (0, 0)))
        reach *= 2
    change = start + jnp.pad(running[:-1], ((1, 0), (0, 0), (0, 0))) - rows_here
    change_sum = jnp.sum(change * change, axis=(1, 2), keepdims=True)
    change_sum = jnp.broadcast_to(change_sum, (z_size, slice_tokens, HD))
    sent = jnp.concatenate([start + running, change_sum], axis=2)
    got = lax.all_to_all(sent, "z", 0, 0)
    new_rows = got[:, :, :block].reshape(token_count, block)
    change_sum = tp_sum(jnp.sum(got[:, 0, block]))
    error_value = change_sum / (token_count * full_width)
    return (new_rows[None], error_value.reshape(1))


def solution(mesh):
    fine = Mesh(mesh.devices.reshape(4, 16, 4, 2), ("x", "z", "y", "core"))
    placed = (
        P(STEP, None, TP),
        P(),
        P(None, TP),
        P(None, TP),
        P(TP),
        P(TP),
        P(STEP, TP),
        P(STEP, TP),
    )
    return jax.shard_map(
        on_device,
        mesh=fine,
        in_specs=placed,
        out_specs=(P(STEP, None, TP), P(STEP)),
        check_vma=False,
    )
```

```python
import math

import jax
import jax.numpy as jnp
from jax import lax
from jax.sharding import Mesh
from jax.sharding import PartitionSpec as P

HD = 128
STEP = ("x", "z")
TP = ("y", "core")

epsilon = 1e-06


def sigma_of(levels):
    scaled = levels.astype(jnp.float32) / 1000.0
    return 5.0 * scaled / (1.0 + 4.0 * scaled)


def tp_sum(value):
    return lax.psum(lax.psum(value, "core"), "y")


def transpose_plane(value):
    side = lax.axis_size("x")
    pairs = [(a * side + b, b * side + a) for a in range(side) for b in range(side)]
    return lax.ppermute(value, ("x", "y"), pairs)


def sum_over(terms, axis):
    size, mine = lax.axis_size(axis), lax.axis_index(axis)
    total = lax.dynamic_index_in_dim(terms, mine, 0, keepdims=False)
    for shift in range(1, size):
        pairs = [(at, (at + shift) % size) for at in range(size)]
        term = lax.dynamic_index_in_dim(terms, (mine + shift) % size, 0, keepdims=False)
        total = total + lax.ppermute(term, axis, pairs)
    return total


def on_device(trajectory, timesteps, context_keys, context_values, ln_gain, q_gain, w_query, w_out):
    latent = trajectory[0]
    token_count, block = latent.shape
    full_width = block * lax.axis_size(TP)
    x_size = lax.axis_size("x")

    z_size = lax.axis_size("z")
    x_here = lax.axis_index("x")
    slice_tokens = token_count // z_size

    depth, cols = w_query.shape
    query_rows = lax.all_to_all(jnp.broadcast_to(w_query, (z_size, depth, cols)), "z", 0, 0)

    sums = jnp.stack([jnp.sum(latent, axis=-1), jnp.sum(latent * latent, axis=-1)])
    sums = tp_sum(sums) / full_width
    row_mean, row_square = sums[0][:, None], sums[1][:, None]
    row_var = row_square - row_mean * row_mean
    normed = ((latent - row_mean) * lax.rsqrt(row_var + epsilon) * ln_gain).astype(jnp.bfloat16)

    w_out, normed = lax.optimization_barrier((w_out, normed))
    out_rows = lax.all_gather(w_out, "x")
    flipped = transpose_plane(normed)
    out_rows, flipped = lax.optimization_barrier((out_rows, flipped))
    out_rows = lax.all_gather(out_rows, "z", axis=1).reshape(-1, block)
    gathered = lax.all_gather(flipped, "y")
    half = x_size // 2
    parts = [lax.all_gather(gathered[at * half : (at + 1) * half], "core") for at in range(2)]
    latent, query_rows, parts = lax.optimization_barrier((latent, query_rows, parts))
    rows_here = lax.all_to_all(latent.reshape(z_size, slice_tokens, block), "z", 0, 0)
    query_weights = query_rows.reshape(2, block, cols)
    partial = [
        jnp.einsum("cxtk,ckn->xtn", part, query_weights, preferred_element_type=jnp.float32)
        for part in parts
    ]
    partial = jnp.concatenate(partial)

    query = sum_over(partial, "x")
    query, rows_here = lax.optimization_barrier((query, rows_here))
    query_width = query.shape[1] * lax.axis_size(TP)
    square_sum = tp_sum(jnp.sum(query * query, axis=-1))
    query_scale = lax.rsqrt(square_sum / query_width + epsilon)[:, None]
    q_normed = (query * query_scale * q_gain).astype(jnp.bfloat16)
    local_heads = query.shape[1] // HD
    q_heads = q_normed.reshape(token_count, local_heads, HD)
    key_heads = context_keys.reshape(context_keys.shape[0], local_heads, HD)
    value_heads = context_values.reshape(context_values.shape[0], local_heads, HD)
    scores = jnp.einsum(
        "thd,khd->htk", q_heads, key_heads, preferred_element_type=jnp.float32
    ) / math.sqrt(HD)
    soft_weights = jax.nn.softmax(scores, axis=-1).astype(jnp.bfloat16)
    attended = jnp.einsum(
        "htk,khd->thd", soft_weights, value_heads, preferred_element_type=jnp.float32
    )
    attended = attended.reshape(token_count, local_heads * HD).astype(jnp.bfloat16)
    attended = attended.reshape(z_size, slice_tokens, -1)
    attended = lax.all_to_all(attended, "z", 0, 0).reshape(token_count, -1)
    later = jnp.concatenate([timesteps[1:], jnp.zeros((1,), timesteps.dtype)])
    step_sizes = sigma_of(later) - sigma_of(timesteps)
    step_sizes = lax.dynamic_slice_in_dim(step_sizes, x_here * z_size, z_size)[:, None, None]

    weighted = jnp.sum(step_sizes * attended.reshape(z_size, slice_tokens, -1), axis=0)
    width = weighted.shape[1]
    sides = lax.all_gather(jnp.concatenate([weighted, rows_here[0]], axis=1), "x")
    weighted = jnp.zeros_like(weighted)
    for at in range(x_size - 1):
        weighted = weighted + jnp.where(at < x_here, sides[at, :, :width], 0.0)
    high = lax.reduce_precision(weighted, 8, 7)
    terms = [high.astype(jnp.bfloat16), (weighted - high).astype(jnp.bfloat16)]
    rows = jnp.concatenate([attended, *terms])

    rows = lax.all_gather(rows, TP, axis=1, tiled=True)
    product = jnp.dot(rows, out_rows, preferred_element_type=jnp.float32)
    velocity = product[:token_count].reshape(z_size, slice_tokens, block)
    terms = product[token_count:].reshape(2, slice_tokens, block)
    start = sides[0, :, width:] + (terms[0] + terms[1])
    drift = step_sizes * velocity

    running = drift
    reach = 1
    while reach < z_size:
        running = running + jnp.pad(running[:-reach], ((reach, 0), (0, 0), (0, 0)))
        reach *= 2
    change = start + jnp.pad(running[:-1], ((1, 0), (0, 0), (0, 0))) - rows_here
    change_sum = jnp.sum(change * change, axis=(1, 2), keepdims=True)
    change_sum = jnp.broadcast_to(change_sum, (z_size, slice_tokens, HD))
    sent = jnp.concatenate([start + running, change_sum], axis=2)
    got = lax.all_to_all(sent, "z", 0, 0)
    new_rows = got[:, :, :block].reshape(token_count, block)
    change_sum = tp_sum(jnp.sum(got[:, 0, block]))
    error_value = change_sum / (token_count * full_width)
    return (new_rows[None], error_value.reshape(1))


def solution(mesh):
    fine = Mesh(mesh.devices.reshape(4, 16, 4, 2), ("x", "z", "y", "core"))
    placed = (
        P(STEP, None, TP),
        P(),
        P(None, TP),
        P(None, TP),
        P(TP),
        P(TP),
        P(STEP, TP),
        P(STEP, TP),
    )
    return jax.shard_map(
        on_device,
        mesh=fine,
        in_specs=placed,
        out_specs=(P(STEP, None, TP), P(STEP)),
        check_vma=False,
    )
```

```python
import math

import jax
import jax.numpy as jnp
from jax import lax
from jax.sharding import Mesh
from jax.sharding import PartitionSpec as P

HD = 128
STEP = ("x", "z")
TP = ("y", "core")

epsilon = 1e-06


def sigma_of(levels):
    scaled = levels.astype(jnp.float32) / 1000.0
    return 5.0 * scaled / (1.0 + 4.0 * scaled)


def tp_sum(value):
    return lax.psum(lax.psum(value, "core"), "y")


def transpose_plane(value):
    side = lax.axis_size("x")
    pairs = [(a * side + b, b * side + a) for a in range(side) for b in range(side)]
    return lax.ppermute(value, ("x", "y"), pairs)


def on_device(trajectory, timesteps, context_keys, context_values, ln_gain, q_gain, w_query, w_out):
    latent = trajectory[0]
    token_count, block = latent.shape
    full_width = block * lax.axis_size(TP)
    x_size = lax.axis_size("x")

    z_size = lax.axis_size("z")
    x_here = lax.axis_index("x")
    slice_tokens = token_count // z_size

    depth, cols = w_query.shape
    query_rows = lax.all_to_all(jnp.broadcast_to(w_query, (z_size, depth, cols)), "z", 0, 0)

    rows_here = lax.all_to_all(latent.reshape(z_size, slice_tokens, block), "z", 0, 0)

    sums = jnp.stack([jnp.sum(latent, axis=-1), jnp.sum(latent * latent, axis=-1)])
    sums = tp_sum(sums) / full_width
    row_mean, row_square = sums[0][:, None], sums[1][:, None]
    row_var = row_square - row_mean * row_mean
    normed = ((latent - row_mean) * lax.rsqrt(row_var + epsilon) * ln_gain).astype(jnp.bfloat16)

    w_out, normed = lax.optimization_barrier((w_out, normed))
    out_rows = lax.all_gather(w_out, "x")
    flipped = transpose_plane(normed)
    out_rows, flipped = lax.optimization_barrier((out_rows, flipped))
    out_rows = lax.all_gather(out_rows, "z", axis=1).reshape(-1, block)
    gathered = lax.all_gather(flipped, "y")
    half = x_size // 2
    parts = [lax.all_gather(gathered[at * half : (at + 1) * half], "core") for at in range(2)]
    query_weights = query_rows.reshape(2, block, cols)
    partial = [
        jnp.einsum("cxtk,ckn->xtn", part, query_weights, preferred_element_type=jnp.float32)
        for part in parts
    ]
    partial = jnp.concatenate(partial)
    query = jnp.sum(lax.all_to_all(partial, "x", 0, 0), axis=0)
    query_width = query.shape[1] * lax.axis_size(TP)
    square_sum = tp_sum(jnp.sum(query * query, axis=-1))
    query_scale = lax.rsqrt(square_sum / query_width + epsilon)[:, None]
    q_normed = (query * query_scale * q_gain).astype(jnp.bfloat16)
    local_heads = query.shape[1] // HD
    q_heads = q_normed.reshape(token_count, local_heads, HD)
    key_heads = context_keys.reshape(context_keys.shape[0], local_heads, HD)
    value_heads = context_values.reshape(context_values.shape[0], local_heads, HD)
    scores = jnp.einsum(
        "thd,khd->htk", q_heads, key_heads, preferred_element_type=jnp.float32
    ) / math.sqrt(HD)
    soft_weights = jax.nn.softmax(scores, axis=-1).astype(jnp.bfloat16)
    attended = jnp.einsum(
        "htk,khd->thd", soft_weights, value_heads, preferred_element_type=jnp.float32
    )
    attended = attended.reshape(token_count, local_heads * HD).astype(jnp.bfloat16)
    attended = attended.reshape(z_size, slice_tokens, -1)
    attended = lax.all_to_all(attended, "z", 0, 0).reshape(token_count, -1)
    attended_all = lax.all_gather(attended, TP, axis=1, tiled=True)
    velocity = jnp.dot(attended_all, out_rows, preferred_element_type=jnp.float32)
    velocity = velocity.reshape(z_size, slice_tokens, block)

    later = jnp.concatenate([timesteps[1:], jnp.zeros((1,), timesteps.dtype)])
    step_sizes = sigma_of(later) - sigma_of(timesteps)
    step_sizes = lax.dynamic_slice_in_dim(step_sizes, x_here * z_size, z_size)
    drift = step_sizes[:, None, None] * velocity

    running = drift
    reach = 1
    while reach < z_size:
        running = running + jnp.pad(running[:-reach], ((reach, 0), (0, 0), (0, 0)))
        reach *= 2
    start = jnp.where(x_here == 0, rows_here[0], 0.0)
    totals = lax.all_gather(running[-1] + start, "x")
    for at in range(x_size - 1):
        start = start + jnp.where(at < x_here, totals[at], 0.0)
    change = start + jnp.pad(running[:-1], ((1, 0), (0, 0), (0, 0))) - rows_here
    change_sum = jnp.sum(change * change, axis=(1, 2), keepdims=True)
    change_sum = jnp.broadcast_to(change_sum, (z_size, slice_tokens, HD))
    sent = jnp.concatenate([start + running, change_sum], axis=2)
    got = lax.all_to_all(sent, "z", 0, 0)
    new_rows = got[:, :, :block].reshape(token_count, block)
    change_sum = tp_sum(jnp.sum(got[:, 0, block]))
    error_value = change_sum / (token_count * full_width)
    return (new_rows[None], error_value.reshape(1))


def solution(mesh):
    fine = Mesh(mesh.devices.reshape(4, 16, 4, 2), ("x", "z", "y", "core"))
    placed = (
        P(STEP, None, TP),
        P(),
        P(None, TP),
        P(None, TP),
        P(TP),
        P(TP),
        P(STEP, TP),
        P(STEP, TP),
    )
    return jax.shard_map(
        on_device,
        mesh=fine,
        in_specs=placed,
        out_specs=(P(STEP, None, TP), P(STEP)),
        check_vma=False,
    )
```

```python
import math

import jax
import jax.numpy as jnp
from jax import lax
from jax.experimental import pallas as pl
from jax.sharding import Mesh
from jax.sharding import PartitionSpec as P

HD = 128
STEP = ("x", "z")
TP = ("y", "core")

epsilon = 1e-06


def sigma_of(levels):
    scaled = levels.astype(jnp.float32) / 1000.0
    return 5.0 * scaled / (1.0 + 4.0 * scaled)


def tp_sum(value):
    return lax.psum(lax.psum(value, "core"), "y")


def transpose_plane(value):
    side = lax.axis_size("x")
    pairs = [(a * side + b, b * side + a) for a in range(side) for b in range(side)]
    return lax.ppermute(value, ("x", "y"), pairs)


def attend_kernel(query, scale, gain, keys, values, attended):
    normed = (query[...] * scale[...] * gain[...]).astype(jnp.bfloat16)
    for head in range(normed.shape[1] // HD):
        part = slice(head * HD, (head + 1) * HD)
        scores = lax.dot_general(
            normed[:, part],
            keys[:, part],
            (((1,), (1,)), ((), ())),
            preferred_element_type=jnp.float32,
        ) / math.sqrt(HD)
        grown = jnp.exp(scores - jnp.max(scores, axis=-1, keepdims=True))
        weights = (grown / jnp.sum(grown, axis=-1, keepdims=True)).astype(jnp.bfloat16)
        got = jnp.dot(weights, values[:, part], preferred_element_type=jnp.float32)
        attended[:, part] = got.astype(jnp.bfloat16)


def attend(query, scale, gain, keys, values):
    return pl.pallas_call(
        attend_kernel,
        out_shape=jax.ShapeDtypeStruct(query.shape, jnp.bfloat16),
        cost_estimate=pl.CostEstimate(flops=20_000_000_000, bytes_accessed=2_000_000, transcendentals=0),
    )(query, scale, gain[None], keys, values)


def on_device(trajectory, timesteps, context_keys, context_values, ln_gain, q_gain, w_query, w_out):
    latent = trajectory[0]
    token_count, block = latent.shape
    full_width = block * lax.axis_size(TP)
    x_size = lax.axis_size("x")

    z_size = lax.axis_size("z")
    x_here = lax.axis_index("x")
    slice_tokens = token_count // z_size

    depth, cols = w_query.shape
    query_rows = lax.all_to_all(jnp.broadcast_to(w_query, (z_size, depth, cols)), "z", 0, 0)

    rows_here = lax.all_to_all(latent.reshape(z_size, slice_tokens, block), "z", 0, 0)

    sums = jnp.stack([jnp.sum(latent, axis=-1), jnp.sum(latent * latent, axis=-1)])
    sums = tp_sum(sums) / full_width
    row_mean, row_square = sums[0][:, None], sums[1][:, None]
    row_var = row_square - row_mean * row_mean
    normed = ((latent - row_mean) * lax.rsqrt(row_var + epsilon) * ln_gain).astype(jnp.bfloat16)

    w_out, normed = lax.optimization_barrier((w_out, normed))
    out_rows = lax.all_gather(w_out, "x")
    flipped = transpose_plane(normed)
    out_rows, flipped = lax.optimization_barrier((out_rows, flipped))
    out_rows = lax.all_gather(out_rows, "z", axis=1).reshape(-1, block)
    gathered = lax.all_gather(flipped, "y")
    half = x_size // 2
    parts = [lax.all_gather(gathered[at * half : (at + 1) * half], "core") for at in range(2)]
    query_weights = query_rows.reshape(2, block, cols)
    partial = [
        jnp.einsum("cxtk,ckn->xtn", part, query_weights, preferred_element_type=jnp.float32)
        for part in parts
    ]
    partial = jnp.concatenate(partial)
    query = jnp.sum(lax.all_to_all(partial, "x", 0, 0), axis=0)
    query_width = query.shape[1] * lax.axis_size(TP)
    square_sum = tp_sum(jnp.sum(query * query, axis=-1))
    query_scale = lax.rsqrt(square_sum / query_width + epsilon)[:, None]
    attended = attend(query, query_scale, q_gain, context_keys, context_values)
    attended = attended.reshape(z_size, slice_tokens, -1)
    attended = lax.all_to_all(attended, "z", 0, 0).reshape(token_count, -1)
    attended_all = lax.all_gather(attended, TP, axis=1, tiled=True)
    velocity = jnp.dot(attended_all, out_rows, preferred_element_type=jnp.float32)
    velocity = velocity.reshape(z_size, slice_tokens, block)

    later = jnp.concatenate([timesteps[1:], jnp.zeros((1,), timesteps.dtype)])
    step_sizes = sigma_of(later) - sigma_of(timesteps)
    step_sizes = lax.dynamic_slice_in_dim(step_sizes, x_here * z_size, z_size)
    drift = step_sizes[:, None, None] * velocity

    running = drift
    reach = 1
    while reach < z_size:
        running = running + jnp.pad(running[:-reach], ((reach, 0), (0, 0), (0, 0)))
        reach *= 2
    start = jnp.where(x_here == 0, rows_here[0], 0.0)
    totals = lax.all_gather(running[-1] + start, "x")
    for at in range(x_size - 1):
        start = start + jnp.where(at < x_here, totals[at], 0.0)
    change = start + jnp.pad(running[:-1], ((1, 0), (0, 0), (0, 0))) - rows_here
    change_sum = jnp.sum(change * change, axis=(1, 2), keepdims=True)
    change_sum = jnp.broadcast_to(change_sum, (z_size, slice_tokens, HD))
    sent = jnp.concatenate([start + running, change_sum], axis=2)
    got = lax.all_to_all(sent, "z", 0, 0)
    new_rows = got[:, :, :block].reshape(token_count, block)
    change_sum = tp_sum(jnp.sum(got[:, 0, block]))
    error_value = change_sum / (token_count * full_width)
    return (new_rows[None], error_value.reshape(1))


def solution(mesh):
    fine = Mesh(mesh.devices.reshape(4, 16, 4, 2), ("x", "z", "y", "core"))
    placed = (
        P(STEP, None, TP),
        P(),
        P(None, TP),
        P(None, TP),
        P(TP),
        P(TP),
        P(STEP, TP),
        P(STEP, TP),
    )
    return jax.shard_map(
        on_device,
        mesh=fine,
        in_specs=placed,
        out_specs=(P(STEP, None, TP), P(STEP)),
        check_vma=False,
    )
```

```python
import math

import jax
import jax.numpy as jnp
from jax import lax
from jax.sharding import Mesh
from jax.sharding import PartitionSpec as P

HD = 128
STEP = ("x", "z")
TP = ("y", "core")

epsilon = 1e-06


def sigma_of(levels):
    scaled = levels.astype(jnp.float32) / 1000.0
    return 5.0 * scaled / (1.0 + 4.0 * scaled)


def tp_sum(value):
    return lax.psum(lax.psum(value, "core"), "y")


def transpose_plane(value):
    side = lax.axis_size("x")
    pairs = [(a * side + b, b * side + a) for a in range(side) for b in range(side)]
    return lax.ppermute(value, ("x", "y"), pairs)


def on_device(trajectory, timesteps, context_keys, context_values, ln_gain, q_gain, w_query, w_out):
    latent = trajectory[0]
    token_count, block = latent.shape
    full_width = block * lax.axis_size(TP)
    x_size = lax.axis_size("x")

    z_size = lax.axis_size("z")
    x_here = lax.axis_index("x")
    slice_tokens = token_count // z_size

    depth, cols = w_query.shape
    both = jnp.concatenate([jnp.pad(w_query, ((0, 0), (0, block - cols))), w_out])
    both = lax.all_gather(both, "z")

    rows_here = lax.all_to_all(latent.reshape(z_size, slice_tokens, block), "z", 0, 0)
    latent = rows_here.reshape(token_count, block)

    sums = jnp.stack([jnp.sum(latent, axis=-1), jnp.sum(latent * latent, axis=-1)])
    sums = tp_sum(sums) / full_width
    row_mean, row_square = sums[0][:, None], sums[1][:, None]
    row_var = row_square - row_mean * row_mean
    normed = ((latent - row_mean) * lax.rsqrt(row_var + epsilon) * ln_gain).astype(jnp.bfloat16)

    flipped = transpose_plane(normed)
    gathered = lax.all_gather(flipped, "y")
    half = x_size // 2
    parts = [lax.all_gather(gathered[at * half : (at + 1) * half], "core") for at in range(2)]
    both, parts = lax.optimization_barrier((both, parts))
    query_weights = both[:, :depth, :cols].reshape(2, block, cols)
    out_rows = both[:, depth:].reshape(-1, block)
    out_rows = lax.all_gather(out_rows, "x", axis=0, tiled=True)
    partial = [
        jnp.einsum("cxtk,ckn->xtn", part, query_weights, preferred_element_type=jnp.float32)
        for part in parts
    ]
    partial = jnp.concatenate(partial)
    query = jnp.sum(lax.all_to_all(partial, "x", 0, 0), axis=0)
    query_width = query.shape[1] * lax.axis_size(TP)
    square_sum = tp_sum(jnp.sum(query * query, axis=-1))
    query_scale = lax.rsqrt(square_sum / query_width + epsilon)[:, None]
    q_normed = (query * query_scale * q_gain).astype(jnp.bfloat16)
    local_heads = query.shape[1] // HD
    q_heads = q_normed.reshape(token_count, local_heads, HD)
    key_heads = context_keys.reshape(context_keys.shape[0], local_heads, HD)
    value_heads = context_values.reshape(context_values.shape[0], local_heads, HD)
    scores = jnp.einsum(
        "thd,khd->htk", q_heads, key_heads, preferred_element_type=jnp.float32
    ) / math.sqrt(HD)
    soft_weights = jax.nn.softmax(scores, axis=-1).astype(jnp.bfloat16)
    attended = jnp.einsum(
        "htk,khd->thd", soft_weights, value_heads, preferred_element_type=jnp.float32
    )
    attended = attended.reshape(token_count, local_heads * HD).astype(jnp.bfloat16)
    attended_all = lax.all_gather(attended, TP, axis=1, tiled=True)
    velocity = jnp.dot(attended_all, out_rows, preferred_element_type=jnp.float32)
    velocity = velocity.reshape(z_size, slice_tokens, block)

    later = jnp.concatenate([timesteps[1:], jnp.zeros((1,), timesteps.dtype)])
    step_sizes = sigma_of(later) - sigma_of(timesteps)
    step_sizes = lax.dynamic_slice_in_dim(step_sizes, x_here * z_size, z_size)
    drift = step_sizes[:, None, None] * velocity

    running = drift
    reach = 1
    while reach < z_size:
        running = running + jnp.pad(running[:-reach], ((reach, 0), (0, 0), (0, 0)))
        reach *= 2
    start = jnp.where(x_here == 0, rows_here[0], 0.0)
    totals = lax.all_gather(running[-1] + start, "x")
    for at in range(x_size - 1):
        start = start + jnp.where(at < x_here, totals[at], 0.0)
    change = start + jnp.pad(running[:-1], ((1, 0), (0, 0), (0, 0))) - rows_here
    change_sum = jnp.sum(change * change, axis=(1, 2), keepdims=True)
    change_sum = jnp.broadcast_to(change_sum, (z_size, slice_tokens, HD))
    sent = jnp.concatenate([start + running, change_sum], axis=2)
    got = lax.all_to_all(sent, "z", 0, 0)
    new_rows = got[:, :, :block].reshape(token_count, block)
    change_sum = tp_sum(jnp.sum(got[:, 0, block]))
    error_value = change_sum / (token_count * full_width)
    return (new_rows[None], error_value.reshape(1))


def solution(mesh):
    fine = Mesh(mesh.devices.reshape(4, 16, 4, 2), ("x", "z", "y", "core"))
    placed = (
        P(STEP, None, TP),
        P(),
        P(None, TP),
        P(None, TP),
        P(TP),
        P(TP),
        P(STEP, TP),
        P(STEP, TP),
    )
    return jax.shard_map(
        on_device,
        mesh=fine,
        in_specs=placed,
        out_specs=(P(STEP, None, TP), P(STEP)),
        check_vma=False,
    )
```

```python
import math

import jax
import jax.numpy as jnp
from jax import lax
from jax.sharding import Mesh
from jax.sharding import PartitionSpec as P

HD = 128
STEP = ("x", "z")
TP = ("y", "core")

epsilon = 1e-06


def sigma_of(levels):
    scaled = levels.astype(jnp.float32) / 1000.0
    return 5.0 * scaled / (1.0 + 4.0 * scaled)


def tp_sum(value):
    return lax.psum(lax.psum(value, "core"), "y")


def transpose_plane(value):
    side = lax.axis_size("x")
    pairs = [(a * side + b, b * side + a) for a in range(side) for b in range(side)]
    return lax.ppermute(value, ("x", "y"), pairs)


def on_device(trajectory, timesteps, context_keys, context_values, ln_gain, q_gain, w_query, w_out):
    latent = trajectory[0]
    token_count, block = latent.shape
    full_width = block * lax.axis_size(TP)
    x_size = lax.axis_size("x")

    z_size = lax.axis_size("z")
    x_here = lax.axis_index("x")
    slice_tokens = token_count // z_size

    depth, cols = w_query.shape
    both = jnp.concatenate([jnp.pad(w_query, ((0, 0), (0, block - cols))), w_out])
    both = lax.all_gather(both, "z")

    rows_here = lax.all_to_all(latent.reshape(z_size, slice_tokens, block), "z", 0, 0)
    latent = rows_here.reshape(token_count, block)

    sums = jnp.stack([jnp.sum(latent, axis=-1), jnp.sum(latent * latent, axis=-1)])
    sums = tp_sum(sums) / full_width
    row_mean, row_square = sums[0][:, None], sums[1][:, None]
    row_var = row_square - row_mean * row_mean
    normed = ((latent - row_mean) * lax.rsqrt(row_var + epsilon) * ln_gain).astype(jnp.bfloat16)

    flipped = transpose_plane(normed)
    gathered = lax.all_gather(flipped, "y")
    half = x_size // 2
    parts = [lax.all_gather(gathered[at * half : (at + 1) * half], "core") for at in range(2)]
    both, parts = lax.optimization_barrier((both, parts))
    query_weights = both[:, :depth, :cols].reshape(2, block, cols)
    partial = [
        jnp.einsum("cxtk,ckn->xtn", part, query_weights, preferred_element_type=jnp.float32)
        for part in parts
    ]
    partial = jnp.concatenate(partial)
    both, partial = lax.optimization_barrier((both, partial))
    out_rows = both[:, depth:].reshape(-1, block)
    out_rows = lax.all_gather(out_rows, "x", axis=0, tiled=True)
    query = jnp.sum(lax.all_to_all(partial, "x", 0, 0), axis=0)
    query_width = query.shape[1] * lax.axis_size(TP)
    square_sum = tp_sum(jnp.sum(query * query, axis=-1))
    query_scale = lax.rsqrt(square_sum / query_width + epsilon)[:, None]
    q_normed = (query * query_scale * q_gain).astype(jnp.bfloat16)
    local_heads = query.shape[1] // HD
    q_heads = q_normed.reshape(token_count, local_heads, HD)
    key_heads = context_keys.reshape(context_keys.shape[0], local_heads, HD)
    value_heads = context_values.reshape(context_values.shape[0], local_heads, HD)
    scores = jnp.einsum(
        "thd,khd->htk", q_heads, key_heads, preferred_element_type=jnp.float32
    ) / math.sqrt(HD)
    soft_weights = jax.nn.softmax(scores, axis=-1).astype(jnp.bfloat16)
    attended = jnp.einsum(
        "htk,khd->thd", soft_weights, value_heads, preferred_element_type=jnp.float32
    )
    attended = attended.reshape(token_count, local_heads * HD).astype(jnp.bfloat16)
    later = jnp.concatenate([timesteps[1:], jnp.zeros((1,), timesteps.dtype)])
    step_sizes = sigma_of(later) - sigma_of(timesteps)
    step_sizes = lax.dynamic_slice_in_dim(step_sizes, x_here * z_size, z_size)[:, None, None]

    weighted = jnp.sum(step_sizes * attended.reshape(z_size, slice_tokens, -1), axis=0)
    width = weighted.shape[1]
    sides = lax.all_gather(jnp.concatenate([weighted, rows_here[0]], axis=1), "x")
    weighted = jnp.zeros_like(weighted)
    for at in range(x_size - 1):
        weighted = weighted + jnp.where(at < x_here, sides[at, :, :width], 0.0)
    high = lax.reduce_precision(weighted, 8, 7)
    terms = [high.astype(jnp.bfloat16), (weighted - high).astype(jnp.bfloat16)]
    rows = jnp.concatenate([attended, *terms])

    rows = lax.all_gather(rows, TP, axis=1, tiled=True)
    product = jnp.dot(rows, out_rows, preferred_element_type=jnp.float32)
    velocity = product[:token_count].reshape(z_size, slice_tokens, block)
    terms = product[token_count:].reshape(2, slice_tokens, block)
    start = sides[0, :, width:] + (terms[0] + terms[1])
    drift = step_sizes * velocity

    running = drift
    reach = 1
    while reach < z_size:
        running = running + jnp.pad(running[:-reach], ((reach, 0), (0, 0), (0, 0)))
        reach *= 2
    change = start + jnp.pad(running[:-1], ((1, 0), (0, 0), (0, 0))) - rows_here
    change_sum = tp_sum(jnp.sum(change * change, axis=(1, 2)))
    change_sum = lax.all_gather(change_sum, "z")
    change_sum = jnp.sum(change_sum, axis=0)[lax.axis_index("z")]
    new_rows = lax.all_to_all(start + running, "z", 0, 0).reshape(token_count, block)
    error_value = change_sum / (token_count * full_width)
    return (new_rows[None], error_value.reshape(1))


def solution(mesh):
    fine = Mesh(mesh.devices.reshape(4, 16, 4, 2), ("x", "z", "y", "core"))
    placed = (
        P(STEP, None, TP),
        P(),
        P(None, TP),
        P(None, TP),
        P(TP),
        P(TP),
        P(STEP, TP),
        P(STEP, TP),
    )
    return jax.shard_map(
        on_device,
        mesh=fine,
        in_specs=placed,
        out_specs=(P(STEP, None, TP), P(STEP)),
        check_vma=False,
    )
```

```python
import math

import jax
import jax.numpy as jnp
from jax import lax
from jax.sharding import Mesh
from jax.sharding import PartitionSpec as P

HD = 128
STEP = ("x", "z")
TP = ("y", "core")

epsilon = 1e-06


def sigma_of(levels):
    scaled = levels.astype(jnp.float32) / 1000.0
    return 5.0 * scaled / (1.0 + 4.0 * scaled)


def tp_sum(value):
    return lax.psum(lax.psum(value, "core"), "y")


def transpose_plane(value):
    side = lax.axis_size("x")
    pairs = [(a * side + b, b * side + a) for a in range(side) for b in range(side)]
    return lax.ppermute(value, ("x", "y"), pairs)


def on_device(trajectory, timesteps, context_keys, context_values, ln_gain, q_gain, w_query, w_out):
    latent = trajectory[0]
    token_count, block = latent.shape
    full_width = block * lax.axis_size(TP)
    x_size = lax.axis_size("x")

    z_size = lax.axis_size("z")
    x_here = lax.axis_index("x")
    slice_tokens = token_count // z_size

    depth, cols = w_query.shape
    both = jnp.concatenate([jnp.pad(w_query, ((0, 0), (0, block - cols))), w_out])
    both = lax.all_gather(both, "z")

    rows_here = lax.all_to_all(latent.reshape(z_size, slice_tokens, block), "z", 0, 0)
    latent = rows_here.reshape(token_count, block)

    sums = jnp.stack([jnp.sum(latent, axis=-1), jnp.sum(latent * latent, axis=-1)])
    sums = tp_sum(sums) / full_width
    row_mean, row_square = sums[0][:, None], sums[1][:, None]
    row_var = row_square - row_mean * row_mean
    normed = ((latent - row_mean) * lax.rsqrt(row_var + epsilon) * ln_gain).astype(jnp.bfloat16)

    flipped = transpose_plane(normed)
    gathered = lax.all_gather(flipped, "y")
    half = x_size // 2
    parts = [lax.all_gather(gathered[at * half : (at + 1) * half], "core") for at in range(2)]
    both, parts = lax.optimization_barrier((both, parts))
    query_weights = both[:, :depth, :cols].reshape(2, block, cols)
    partial = [
        jnp.einsum("cxtk,ckn->xtn", part, query_weights, preferred_element_type=jnp.float32)
        for part in parts
    ]
    partial = jnp.concatenate(partial)
    both, partial = lax.optimization_barrier((both, partial))
    out_rows = both[:, depth:].reshape(-1, block)
    out_rows = lax.all_gather(out_rows, "x", axis=0, tiled=True)
    query = jnp.sum(lax.all_to_all(partial, "x", 0, 0), axis=0)
    query_width = query.shape[1] * lax.axis_size(TP)
    square_sum = tp_sum(jnp.sum(query * query, axis=-1))
    query_scale = lax.rsqrt(square_sum / query_width + epsilon)[:, None]
    q_normed = (query * query_scale * q_gain).astype(jnp.bfloat16)
    local_heads = query.shape[1] // HD
    q_heads = q_normed.reshape(token_count, local_heads, HD)
    key_heads = context_keys.reshape(context_keys.shape[0], local_heads, HD)
    value_heads = context_values.reshape(context_values.shape[0], local_heads, HD)
    scores = jnp.einsum(
        "thd,khd->htk", q_heads, key_heads, preferred_element_type=jnp.float32
    ) / math.sqrt(HD)
    soft_weights = jax.nn.softmax(scores, axis=-1).astype(jnp.bfloat16)
    attended = jnp.einsum(
        "htk,khd->thd", soft_weights, value_heads, preferred_element_type=jnp.float32
    )
    attended = attended.reshape(token_count, local_heads * HD).astype(jnp.bfloat16)
    later = jnp.concatenate([timesteps[1:], jnp.zeros((1,), timesteps.dtype)])
    step_sizes = sigma_of(later) - sigma_of(timesteps)
    step_sizes = lax.dynamic_slice_in_dim(step_sizes, x_here * z_size, z_size)[:, None, None]

    weighted = jnp.sum(step_sizes * attended.reshape(z_size, slice_tokens, -1), axis=0)
    width = weighted.shape[1]
    sides = lax.all_gather(jnp.concatenate([weighted, rows_here[0]], axis=1), "x")
    weighted = jnp.zeros_like(weighted)
    for at in range(x_size - 1):
        weighted = weighted + jnp.where(at < x_here, sides[at, :, :width], 0.0)
    high = lax.reduce_precision(weighted, 8, 7)
    terms = [high.astype(jnp.bfloat16), (weighted - high).astype(jnp.bfloat16)]
    rows = jnp.concatenate([attended, *terms])

    rows = lax.all_gather(rows, TP, axis=1, tiled=True)
    product = jnp.dot(rows, out_rows, preferred_element_type=jnp.float32)
    velocity = product[:token_count].reshape(z_size, slice_tokens, block)
    terms = product[token_count:].reshape(2, slice_tokens, block)
    start = sides[0, :, width:] + (terms[0] + terms[1])
    drift = step_sizes * velocity

    running = drift
    reach = 1
    while reach < z_size:
        running = running + jnp.pad(running[:-reach], ((reach, 0), (0, 0), (0, 0)))
        reach *= 2
    change = start + jnp.pad(running[:-1], ((1, 0), (0, 0), (0, 0))) - rows_here
    change_sum = tp_sum(jnp.sum(change * change, axis=(1, 2)))
    new_rows = lax.all_to_all(start + running, "z", 0, 0).reshape(token_count, block)
    change_sum, new_rows = lax.optimization_barrier((change_sum, new_rows))
    change_sum = jnp.broadcast_to(change_sum[:, None, None], (z_size, 1, HD))
    change_sum = jnp.sum(lax.all_to_all(change_sum, "z", 0, 0)[:, 0, 0])
    error_value = change_sum / (token_count * full_width)
    return (new_rows[None], error_value.reshape(1))


def solution(mesh):
    fine = Mesh(mesh.devices.reshape(4, 16, 4, 2), ("x", "z", "y", "core"))
    placed = (
        P(STEP, None, TP),
        P(),
        P(None, TP),
        P(None, TP),
        P(TP),
        P(TP),
        P(STEP, TP),
        P(STEP, TP),
    )
    return jax.shard_map(
        on_device,
        mesh=fine,
        in_specs=placed,
        out_specs=(P(STEP, None, TP), P(STEP)),
        check_vma=False,
    )
```

```python
import math

import jax
import jax.numpy as jnp
from jax import lax
from jax.experimental import pallas as pl
from jax.sharding import Mesh
from jax.sharding import PartitionSpec as P

HD = 128
STEP = ("x", "z")
TP = ("y", "core")

epsilon = 1e-06


def sigma_of(levels):
    scaled = levels.astype(jnp.float32) / 1000.0
    return 5.0 * scaled / (1.0 + 4.0 * scaled)


def tp_sum(value):
    return lax.psum(lax.psum(value, "core"), "y")


def transpose_plane(value):
    side = lax.axis_size("x")
    pairs = [(a * side + b, b * side + a) for a in range(side) for b in range(side)]
    return lax.ppermute(value, ("x", "y"), pairs)


def side_kernel(sizes, attended, first, side):
    rows, width = first.shape[0], attended.shape[1]
    weighted = sizes[...] * attended[...].astype(jnp.float32)
    side[:, :width] = jnp.sum(weighted.reshape(-1, rows, width), axis=0)
    side[:, width:] = first[...]


def weighted_side(sizes, attended, first):
    shape = (first.shape[0], attended.shape[1] + first.shape[1])
    return pl.pallas_call(
        side_kernel,
        out_shape=jax.ShapeDtypeStruct(shape, jnp.float32),
        cost_estimate=pl.CostEstimate(flops=50_000_000_000, bytes_accessed=1_000_000, transcendentals=0),
    )(sizes, attended, first)


def on_device(trajectory, timesteps, context_keys, context_values, ln_gain, q_gain, w_query, w_out):
    latent = trajectory[0]
    token_count, block = latent.shape
    full_width = block * lax.axis_size(TP)
    x_size = lax.axis_size("x")

    z_size = lax.axis_size("z")
    x_here = lax.axis_index("x")
    slice_tokens = token_count // z_size

    depth, cols = w_query.shape
    both = jnp.concatenate([jnp.pad(w_query, ((0, 0), (0, block - cols))), w_out])
    both = lax.all_gather(both, "z")

    rows_here = lax.all_to_all(latent.reshape(z_size, slice_tokens, block), "z", 0, 0)
    latent = rows_here.reshape(token_count, block)

    sums = jnp.stack([jnp.sum(latent, axis=-1), jnp.sum(latent * latent, axis=-1)])
    sums = tp_sum(sums) / full_width
    row_mean, row_square = sums[0][:, None], sums[1][:, None]
    row_var = row_square - row_mean * row_mean
    normed = ((latent - row_mean) * lax.rsqrt(row_var + epsilon) * ln_gain).astype(jnp.bfloat16)

    flipped = transpose_plane(normed)
    gathered = lax.all_gather(flipped, "y")
    half = x_size // 2
    parts = [lax.all_gather(gathered[at * half : (at + 1) * half], "core") for at in range(2)]
    both, parts = lax.optimization_barrier((both, parts))
    query_weights = both[:, :depth, :cols].reshape(2, block, cols)
    partial = [
        jnp.einsum("cxtk,ckn->xtn", part, query_weights, preferred_element_type=jnp.float32)
        for part in parts
    ]
    partial = jnp.concatenate(partial)
    both, partial = lax.optimization_barrier((both, partial))
    out_rows = both[:, depth:].reshape(-1, block)
    out_rows = lax.all_gather(out_rows, "x", axis=0, tiled=True)
    query = jnp.sum(lax.all_to_all(partial, "x", 0, 0), axis=0)
    query_width = query.shape[1] * lax.axis_size(TP)
    square_sum = tp_sum(jnp.sum(query * query, axis=-1))
    query_scale = lax.rsqrt(square_sum / query_width + epsilon)[:, None]
    q_normed = (query * query_scale * q_gain).astype(jnp.bfloat16)
    local_heads = query.shape[1] // HD
    q_heads = q_normed.reshape(token_count, local_heads, HD)
    key_heads = context_keys.reshape(context_keys.shape[0], local_heads, HD)
    value_heads = context_values.reshape(context_values.shape[0], local_heads, HD)
    scores = jnp.einsum(
        "thd,khd->htk", q_heads, key_heads, preferred_element_type=jnp.float32
    ) / math.sqrt(HD)
    soft_weights = jax.nn.softmax(scores, axis=-1).astype(jnp.bfloat16)
    attended = jnp.einsum(
        "htk,khd->thd", soft_weights, value_heads, preferred_element_type=jnp.float32
    )
    attended = attended.reshape(token_count, local_heads * HD).astype(jnp.bfloat16)
    later = jnp.concatenate([timesteps[1:], jnp.zeros((1,), timesteps.dtype)])
    step_sizes = sigma_of(later) - sigma_of(timesteps)
    step_sizes = lax.dynamic_slice_in_dim(step_sizes, x_here * z_size, z_size)[:, None, None]

    width = attended.shape[1]
    row_sizes = jnp.broadcast_to(step_sizes, (z_size, slice_tokens, 1)).reshape(token_count, 1)
    sides = lax.all_gather(weighted_side(row_sizes, attended, rows_here[0]), "x")
    weighted = jnp.zeros((slice_tokens, width), jnp.float32)
    for at in range(x_size - 1):
        weighted = weighted + jnp.where(at < x_here, sides[at, :, :width], 0.0)
    high = lax.reduce_precision(weighted, 8, 7)
    terms = [high.astype(jnp.bfloat16), (weighted - high).astype(jnp.bfloat16)]
    rows = jnp.concatenate([attended, *terms])

    rows = lax.all_gather(rows, TP, axis=1, tiled=True)
    product = jnp.dot(rows, out_rows, preferred_element_type=jnp.float32)
    velocity = product[:token_count].reshape(z_size, slice_tokens, block)
    terms = product[token_count:].reshape(2, slice_tokens, block)
    start = sides[0, :, width:] + (terms[0] + terms[1])
    drift = step_sizes * velocity

    running = drift
    reach = 1
    while reach < z_size:
        running = running + jnp.pad(running[:-reach], ((reach, 0), (0, 0), (0, 0)))
        reach *= 2
    change = start + jnp.pad(running[:-1], ((1, 0), (0, 0), (0, 0))) - rows_here
    change_sum = jnp.sum(change * change, axis=(1, 2), keepdims=True)
    change_sum = jnp.broadcast_to(change_sum, (z_size, slice_tokens, HD))
    sent = jnp.concatenate([start + running, change_sum], axis=2)
    got = lax.all_to_all(sent, "z", 0, 0)
    new_rows = got[:, :, :block].reshape(token_count, block)
    change_sum = tp_sum(jnp.sum(got[:, 0, block]))
    error_value = change_sum / (token_count * full_width)
    return (new_rows[None], error_value.reshape(1))


def solution(mesh):
    fine = Mesh(mesh.devices.reshape(4, 16, 4, 2), ("x", "z", "y", "core"))
    placed = (
        P(STEP, None, TP),
        P(),
        P(None, TP),
        P(None, TP),
        P(TP),
        P(TP),
        P(STEP, TP),
        P(STEP, TP),
    )
    return jax.shard_map(
        on_device,
        mesh=fine,
        in_specs=placed,
        out_specs=(P(STEP, None, TP), P(STEP)),
        check_vma=False,
    )
```

```python
import math

import jax
import jax.numpy as jnp
from jax import lax
from jax.sharding import Mesh
from jax.sharding import PartitionSpec as P

HD = 128
STEP = ("x", "z")
TP = ("y", "core")

epsilon = 1e-06


def sigma_of(levels):
    scaled = levels.astype(jnp.float32) / 1000.0
    return 5.0 * scaled / (1.0 + 4.0 * scaled)


def tp_sum(value):
    return lax.psum(lax.psum(value, "core"), "y")


def transpose_plane(value):
    side = lax.axis_size("x")
    pairs = [(a * side + b, b * side + a) for a in range(side) for b in range(side)]
    return lax.ppermute(value, ("x", "y"), pairs)


def on_device(trajectory, timesteps, context_keys, context_values, ln_gain, q_gain, w_query, w_out):
    latent = trajectory[0]
    token_count, block = latent.shape
    full_width = block * lax.axis_size(TP)
    x_size = lax.axis_size("x")

    z_size = lax.axis_size("z")
    x_here = lax.axis_index("x")
    slice_tokens = token_count // z_size

    depth, cols = w_query.shape
    both = jnp.concatenate([jnp.pad(w_query, ((0, 0), (0, block - cols))), w_out])
    both = lax.all_gather(both, "z")

    rows_here = lax.all_to_all(latent.reshape(z_size, slice_tokens, block), "z", 0, 0)
    latent = rows_here.reshape(token_count, block)

    sums = jnp.stack([jnp.sum(latent, axis=-1), jnp.sum(latent * latent, axis=-1)])
    sums = tp_sum(sums) / full_width
    row_mean, row_square = sums[0][:, None], sums[1][:, None]
    row_var = row_square - row_mean * row_mean
    normed = ((latent - row_mean) * lax.rsqrt(row_var + epsilon) * ln_gain).astype(jnp.bfloat16)

    flipped = transpose_plane(normed)
    gathered = lax.all_gather(flipped, "y")
    half = x_size // 2
    parts = [lax.all_gather(gathered[at * half : (at + 1) * half], "core") for at in range(2)]
    both, parts = lax.optimization_barrier((both, parts))
    query_weights = both[:, :depth, :cols].reshape(2, block, cols)
    out_rows = both[:, depth:].reshape(-1, block)
    out_rows = lax.all_gather(out_rows, "x", axis=0, tiled=True)
    partial = [
        jnp.einsum("cxtk,ckn->xtn", part, query_weights, preferred_element_type=jnp.float32)
        for part in parts
    ]
    partial = jnp.concatenate(partial)
    query = jnp.sum(lax.all_to_all(partial, "x", 0, 0), axis=0)
    query_width = query.shape[1] * lax.axis_size(TP)
    square_sum = tp_sum(jnp.sum(query * query, axis=-1))
    query_scale = lax.rsqrt(square_sum / query_width + epsilon)[:, None]
    q_normed = (query * query_scale * q_gain).astype(jnp.bfloat16)
    local_heads = query.shape[1] // HD
    q_heads = q_normed.reshape(token_count, local_heads, HD)
    key_heads = context_keys.reshape(context_keys.shape[0], local_heads, HD)
    value_heads = context_values.reshape(context_values.shape[0], local_heads, HD)
    scores = jnp.einsum(
        "thd,khd->htk", q_heads, key_heads, preferred_element_type=jnp.float32
    ) / math.sqrt(HD)
    soft_weights = jax.nn.softmax(scores, axis=-1).astype(jnp.bfloat16)
    attended = jnp.einsum(
        "htk,khd->thd", soft_weights, value_heads, preferred_element_type=jnp.float32
    )
    attended = attended.reshape(token_count, local_heads * HD).astype(jnp.bfloat16)
    later = jnp.concatenate([timesteps[1:], jnp.zeros((1,), timesteps.dtype)])
    step_sizes = sigma_of(later) - sigma_of(timesteps)
    step_sizes = lax.dynamic_slice_in_dim(step_sizes, x_here * z_size, z_size)[:, None, None]

    weighted = jnp.sum(step_sizes * attended.reshape(z_size, slice_tokens, -1), axis=0)
    width = weighted.shape[1]
    sides = lax.all_gather(jnp.concatenate([weighted, rows_here[0]], axis=1), "x")
    weighted = jnp.zeros_like(weighted)
    for at in range(x_size - 1):
        weighted = weighted + jnp.where(at < x_here, sides[at, :, :width], 0.0)
    high = lax.reduce_precision(weighted, 8, 7)
    terms = [high.astype(jnp.bfloat16), (weighted - high).astype(jnp.bfloat16)]
    rows = jnp.concatenate([attended, *terms])

    rows = lax.all_gather(rows, TP, axis=1, tiled=True)
    product = jnp.dot(rows, out_rows, preferred_element_type=jnp.float32)
    velocity = product[:token_count].reshape(z_size, slice_tokens, block)
    terms = product[token_count:].reshape(2, slice_tokens, block)
    start = sides[0, :, width:] + (terms[0] + terms[1])
    drift = step_sizes * velocity

    running = drift
    reach = 1
    while reach < z_size:
        running = running + jnp.pad(running[:-reach], ((reach, 0), (0, 0), (0, 0)))
        reach *= 2
    change = start + jnp.pad(running[:-1], ((1, 0), (0, 0), (0, 0))) - rows_here
    change_sum = jnp.sum(change * change, axis=(1, 2), keepdims=True)
    change_sum = jnp.broadcast_to(change_sum, (z_size, slice_tokens, HD))
    sent = jnp.concatenate([start + running, change_sum], axis=2)
    got = lax.all_to_all(sent, "z", 0, 0)
    new_rows = got[:, :, :block].reshape(token_count, block)
    change_sum = tp_sum(jnp.sum(got[:, 0, block]))
    error_value = change_sum / (token_count * full_width)
    return (new_rows[None], error_value.reshape(1))


def solution(mesh):
    fine = Mesh(mesh.devices.reshape(4, 16, 4, 2), ("x", "z", "y", "core"))
    placed = (
        P(STEP, None, TP),
        P(),
        P(None, TP),
        P(None, TP),
        P(TP),
        P(TP),
        P(STEP, TP),
        P(STEP, TP),
    )
    return jax.shard_map(
        on_device,
        mesh=fine,
        in_specs=placed,
        out_specs=(P(STEP, None, TP), P(STEP)),
        check_vma=False,
    )
```

```python
import math

import jax
import jax.numpy as jnp
from jax import lax
from jax.sharding import Mesh
from jax.sharding import PartitionSpec as P

HD = 128
STEP = ("x", "z")
TP = ("y", "core")

epsilon = 1e-06


def sigma_of(levels):
    scaled = levels.astype(jnp.float32) / 1000.0
    return 5.0 * scaled / (1.0 + 4.0 * scaled)


def tp_sum(value):
    return lax.psum(lax.psum(value, "core"), "y")


def transpose_plane(value):
    side = lax.axis_size("x")
    pairs = [(a * side + b, b * side + a) for a in range(side) for b in range(side)]
    return lax.ppermute(value, ("x", "y"), pairs)


def on_device(trajectory, timesteps, context_keys, context_values, ln_gain, q_gain, w_query, w_out):
    latent = trajectory[0]
    token_count, block = latent.shape
    full_width = block * lax.axis_size(TP)
    x_size = lax.axis_size("x")

    z_size = lax.axis_size("z")
    x_here = lax.axis_index("x")
    slice_tokens = token_count // z_size

    depth, cols = w_query.shape
    both = jnp.concatenate([jnp.pad(w_query, ((0, 0), (0, block - cols))), w_out])
    both = lax.all_gather(both, "z")

    rows_here = lax.all_to_all(latent.reshape(z_size, slice_tokens, block), "z", 0, 0)
    latent = rows_here.reshape(token_count, block)

    sums = jnp.stack([jnp.sum(latent, axis=-1), jnp.sum(latent * latent, axis=-1)])
    sums = tp_sum(sums) / full_width
    row_mean, row_square = sums[0][:, None], sums[1][:, None]
    row_var = row_square - row_mean * row_mean
    normed = ((latent - row_mean) * lax.rsqrt(row_var + epsilon) * ln_gain).astype(jnp.bfloat16)

    flipped = transpose_plane(normed)
    gathered = lax.all_gather(flipped, "y")
    half = x_size // 2
    parts = [lax.all_gather(gathered[at * half : (at + 1) * half], "core") for at in range(2)]
    both, parts = lax.optimization_barrier((both, parts))
    query_weights = both[:, :depth, :cols].reshape(2, block, cols)
    out_rows = both[:, depth:].reshape(-1, block)
    out_rows = lax.all_gather(out_rows, "x", axis=0, tiled=True)
    partial = [
        jnp.einsum("cxtk,ckn->xtn", part, query_weights, preferred_element_type=jnp.float32)
        for part in parts
    ]
    partial = jnp.concatenate(partial)
    query = jnp.sum(lax.all_to_all(partial, "x", 0, 0), axis=0)
    query_width = query.shape[1] * lax.axis_size(TP)
    square_sum = tp_sum(jnp.sum(query * query, axis=-1))
    query_scale = lax.rsqrt(square_sum / query_width + epsilon)[:, None]
    q_normed = (query * query_scale * q_gain).astype(jnp.bfloat16)
    local_heads = query.shape[1] // HD
    q_heads = q_normed.reshape(token_count, local_heads, HD)
    key_heads = context_keys.reshape(context_keys.shape[0], local_heads, HD)
    value_heads = context_values.reshape(context_values.shape[0], local_heads, HD)
    scores = jnp.einsum(
        "thd,khd->htk", q_heads, key_heads, preferred_element_type=jnp.float32
    ) / math.sqrt(HD)
    soft_weights = jax.nn.softmax(scores, axis=-1).astype(jnp.bfloat16)
    attended = jnp.einsum(
        "htk,khd->thd", soft_weights, value_heads, preferred_element_type=jnp.float32
    )
    attended = attended.reshape(token_count, local_heads * HD).astype(jnp.bfloat16)
    attended = lax.optimization_barrier(attended)

    later = jnp.concatenate([timesteps[1:], jnp.zeros((1,), timesteps.dtype)])
    step_sizes = sigma_of(later) - sigma_of(timesteps)
    step_sizes = lax.dynamic_slice_in_dim(step_sizes, x_here * z_size, z_size)[:, None, None]

    weighted = jnp.sum(step_sizes * attended.reshape(z_size, slice_tokens, -1), axis=0)
    width = weighted.shape[1]
    sides = lax.all_gather(jnp.concatenate([weighted, rows_here[0]], axis=1), "x")
    weighted = jnp.zeros_like(weighted)
    for at in range(x_size - 1):
        weighted = weighted + jnp.where(at < x_here, sides[at, :, :width], 0.0)
    high = lax.reduce_precision(weighted, 8, 7)
    terms = [high.astype(jnp.bfloat16), (weighted - high).astype(jnp.bfloat16)]
    rows = jnp.concatenate([attended, *terms])

    rows = lax.all_gather(rows, TP, axis=1, tiled=True)
    product = jnp.dot(rows, out_rows, preferred_element_type=jnp.float32)
    velocity = product[:token_count].reshape(z_size, slice_tokens, block)
    terms = product[token_count:].reshape(2, slice_tokens, block)
    start = sides[0, :, width:] + (terms[0] + terms[1])
    drift = step_sizes * velocity

    running = drift
    reach = 1
    while reach < z_size:
        running = running + jnp.pad(running[:-reach], ((reach, 0), (0, 0), (0, 0)))
        reach *= 2
    change = start + jnp.pad(running[:-1], ((1, 0), (0, 0), (0, 0))) - rows_here
    change_sum = jnp.sum(change * change, axis=(1, 2), keepdims=True)
    change_sum = jnp.broadcast_to(change_sum, (z_size, slice_tokens, HD))
    sent = jnp.concatenate([start + running, change_sum], axis=2)
    got = lax.all_to_all(sent, "z", 0, 0)
    new_rows = got[:, :, :block].reshape(token_count, block)
    change_sum = tp_sum(jnp.sum(got[:, 0, block]))
    error_value = change_sum / (token_count * full_width)
    return (new_rows[None], error_value.reshape(1))


def solution(mesh):
    fine = Mesh(mesh.devices.reshape(4, 16, 4, 2), ("x", "z", "y", "core"))
    placed = (
        P(STEP, None, TP),
        P(),
        P(None, TP),
        P(None, TP),
        P(TP),
        P(TP),
        P(STEP, TP),
        P(STEP, TP),
    )
    return jax.shard_map(
        on_device,
        mesh=fine,
        in_specs=placed,
        out_specs=(P(STEP, None, TP), P(STEP)),
        check_vma=False,
    )
```

```python
import math

import jax
import jax.numpy as jnp
from jax import lax
from jax.sharding import Mesh
from jax.sharding import PartitionSpec as P

HD = 128
STEP = ("x", "z")
TP = ("y", "core")

epsilon = 1e-06


def sigma_of(levels):
    scaled = levels.astype(jnp.float32) / 1000.0
    return 5.0 * scaled / (1.0 + 4.0 * scaled)


def tp_sum(value):
    return lax.psum(lax.psum(value, "core"), "y")


def transpose_plane(value):
    side = lax.axis_size("x")
    pairs = [(a * side + b, b * side + a) for a in range(side) for b in range(side)]
    return lax.ppermute(value, ("x", "y"), pairs)


def on_device(trajectory, timesteps, context_keys, context_values, ln_gain, q_gain, w_query, w_out):
    latent = trajectory[0]
    token_count, block = latent.shape
    full_width = block * lax.axis_size(TP)
    x_size = lax.axis_size("x")

    z_size = lax.axis_size("z")
    x_here = lax.axis_index("x")
    slice_tokens = token_count // z_size

    depth, cols = w_query.shape
    both = jnp.concatenate([jnp.pad(w_query, ((0, 0), (0, block - cols))), w_out])
    both = lax.all_gather(both, "z")

    rows_here = lax.all_to_all(latent.reshape(z_size, slice_tokens, block), "z", 0, 0)
    latent = rows_here.reshape(token_count, block)

    sums = jnp.stack([jnp.sum(latent, axis=-1), jnp.sum(latent * latent, axis=-1)])
    sums = tp_sum(sums) / full_width
    row_mean, row_square = sums[0][:, None], sums[1][:, None]
    row_var = row_square - row_mean * row_mean
    normed = ((latent - row_mean) * lax.rsqrt(row_var + epsilon) * ln_gain).astype(jnp.bfloat16)

    flipped = transpose_plane(normed)
    gathered = lax.all_gather(flipped, "y")
    parts = [lax.all_gather(gathered[:, :, :cols], "core"), lax.all_gather(gathered[:, :, cols:], "core")]
    both, parts = lax.optimization_barrier((both, parts))
    query_weights = both[:, :depth, :cols].reshape(2, block, cols)
    out_rows = both[:, depth:].reshape(-1, block)
    out_rows = lax.all_gather(out_rows, "x", axis=0, tiled=True)
    partial = 0.0
    for part, weights in zip(parts, (query_weights[:, :cols], query_weights[:, cols:])):
        partial += jnp.einsum("cxtk,ckn->xtn", part, weights, preferred_element_type=jnp.float32)
    query = jnp.sum(lax.all_to_all(partial, "x", 0, 0), axis=0)
    query_width = query.shape[1] * lax.axis_size(TP)
    square_sum = tp_sum(jnp.sum(query * query, axis=-1))
    query_scale = lax.rsqrt(square_sum / query_width + epsilon)[:, None]
    q_normed = (query * query_scale * q_gain).astype(jnp.bfloat16)
    local_heads = query.shape[1] // HD
    q_heads = q_normed.reshape(token_count, local_heads, HD)
    key_heads = context_keys.reshape(context_keys.shape[0], local_heads, HD)
    value_heads = context_values.reshape(context_values.shape[0], local_heads, HD)
    scores = jnp.einsum(
        "thd,khd->htk", q_heads, key_heads, preferred_element_type=jnp.float32
    ) / math.sqrt(HD)
    soft_weights = jax.nn.softmax(scores, axis=-1).astype(jnp.bfloat16)
    attended = jnp.einsum(
        "htk,khd->thd", soft_weights, value_heads, preferred_element_type=jnp.float32
    )
    attended = attended.reshape(token_count, local_heads * HD).astype(jnp.bfloat16)
    attended = lax.optimization_barrier(attended)

    later = jnp.concatenate([timesteps[1:], jnp.zeros((1,), timesteps.dtype)])
    step_sizes = sigma_of(later) - sigma_of(timesteps)
    step_sizes = lax.dynamic_slice_in_dim(step_sizes, x_here * z_size, z_size)[:, None, None]

    weighted = jnp.sum(step_sizes * attended.reshape(z_size, slice_tokens, -1), axis=0)
    width = weighted.shape[1]
    sides = lax.all_gather(jnp.concatenate([weighted, rows_here[0]], axis=1), "x")
    weighted = jnp.zeros_like(weighted)
    for at in range(x_size - 1):
        weighted = weighted + jnp.where(at < x_here, sides[at, :, :width], 0.0)
    high = lax.reduce_precision(weighted, 8, 7)
    terms = [high.astype(jnp.bfloat16), (weighted - high).astype(jnp.bfloat16)]
    rows = jnp.concatenate([attended, *terms])

    rows = lax.all_gather(rows, TP, axis=1, tiled=True)
    product = jnp.dot(rows, out_rows, preferred_element_type=jnp.float32)
    velocity = product[:token_count].reshape(z_size, slice_tokens, block)
    terms = product[token_count:].reshape(2, slice_tokens, block)
    start = sides[0, :, width:] + (terms[0] + terms[1])
    drift = step_sizes * velocity

    running = drift
    reach = 1
    while reach < z_size:
        running = running + jnp.pad(running[:-reach], ((reach, 0), (0, 0), (0, 0)))
        reach *= 2
    change = start + jnp.pad(running[:-1], ((1, 0), (0, 0), (0, 0))) - rows_here
    change_sum = jnp.sum(change * change, axis=(1, 2), keepdims=True)
    change_sum = jnp.broadcast_to(change_sum, (z_size, slice_tokens, HD))
    sent = jnp.concatenate([start + running, change_sum], axis=2)
    got = lax.all_to_all(sent, "z", 0, 0)
    new_rows = got[:, :, :block].reshape(token_count, block)
    change_sum = tp_sum(jnp.sum(got[:, 0, block]))
    error_value = change_sum / (token_count * full_width)
    return (new_rows[None], error_value.reshape(1))


def solution(mesh):
    fine = Mesh(mesh.devices.reshape(4, 16, 4, 2), ("x", "z", "y", "core"))
    placed = (
        P(STEP, None, TP),
        P(),
        P(None, TP),
        P(None, TP),
        P(TP),
        P(TP),
        P(STEP, TP),
        P(STEP, TP),
    )
    return jax.shard_map(
        on_device,
        mesh=fine,
        in_specs=placed,
        out_specs=(P(STEP, None, TP), P(STEP)),
        check_vma=False,
    )
```

```python
import math

import jax
import jax.numpy as jnp
from jax import lax
from jax.sharding import Mesh
from jax.sharding import PartitionSpec as P

HD = 128
STEP = ("x", "z")
TP = ("y", "core")

epsilon = 1e-06


def sigma_of(levels):
    scaled = levels.astype(jnp.float32) / 1000.0
    return 5.0 * scaled / (1.0 + 4.0 * scaled)


def tp_sum(value):
    return lax.psum(lax.psum(value, "core"), "y")


def transpose_plane(value):
    side = lax.axis_size("x")
    pairs = [(a * side + b, b * side + a) for a in range(side) for b in range(side)]
    return lax.ppermute(value, ("x", "y"), pairs)


def on_device(trajectory, timesteps, context_keys, context_values, ln_gain, q_gain, w_query, w_out):
    latent = trajectory[0]
    token_count, block = latent.shape
    full_width = block * lax.axis_size(TP)
    x_size = lax.axis_size("x")

    z_size = lax.axis_size("z")
    x_here = lax.axis_index("x")
    slice_tokens = token_count // z_size

    depth, cols = w_query.shape
    both = jnp.concatenate([jnp.pad(w_query, ((0, 0), (0, block - cols))), w_out])
    both = lax.all_gather(both, "z")

    rows_here = lax.all_to_all(latent.reshape(z_size, slice_tokens, block), "z", 0, 0)
    latent = rows_here.reshape(token_count, block)

    sums = jnp.stack([jnp.sum(latent, axis=-1), jnp.sum(latent * latent, axis=-1)])
    sums = tp_sum(sums) / full_width
    row_mean, row_square = sums[0][:, None], sums[1][:, None]
    row_var = row_square - row_mean * row_mean
    normed = ((latent - row_mean) * lax.rsqrt(row_var + epsilon) * ln_gain).astype(jnp.bfloat16)

    flipped = transpose_plane(normed)
    gathered = lax.all_gather(flipped, "y")
    parts = [lax.all_gather(gathered[:, :, :cols], "core"), lax.all_gather(gathered[:, :, cols:], "core")]
    both, parts = lax.optimization_barrier((both, parts))
    query_weights = both[:, :depth, :cols].reshape(2, block, cols)
    out_rows = both[:, depth:].reshape(-1, block)
    out_rows = lax.all_gather(out_rows, "x", axis=0, tiled=True)
    partial = 0.0
    for part, weights in zip(parts, (query_weights[:, :cols], query_weights[:, cols:])):
        partial += jnp.einsum("cxtk,ckn->xtn", part, weights, preferred_element_type=jnp.float32)
    query = jnp.sum(lax.all_to_all(partial, "x", 0, 0), axis=0)
    query_width = query.shape[1] * lax.axis_size(TP)
    square_sum = tp_sum(jnp.sum(query * query, axis=-1))
    query_scale = lax.rsqrt(square_sum / query_width + epsilon)[:, None]
    q_normed = (query * query_scale * q_gain).astype(jnp.bfloat16)
    local_heads = query.shape[1] // HD
    q_heads = q_normed.reshape(token_count, local_heads, HD)
    key_heads = context_keys.reshape(context_keys.shape[0], local_heads, HD)
    value_heads = context_values.reshape(context_values.shape[0], local_heads, HD)
    scores = jnp.einsum(
        "thd,khd->htk", q_heads, key_heads, preferred_element_type=jnp.float32
    ) / math.sqrt(HD)
    soft_weights = jax.nn.softmax(scores, axis=-1).astype(jnp.bfloat16)
    attended = jnp.einsum(
        "htk,khd->thd", soft_weights, value_heads, preferred_element_type=jnp.float32
    )
    attended = attended.reshape(token_count, local_heads * HD).astype(jnp.bfloat16)
    attended = lax.optimization_barrier(attended)

    later = jnp.concatenate([timesteps[1:], jnp.zeros((1,), timesteps.dtype)])
    step_sizes = sigma_of(later) - sigma_of(timesteps)
    step_sizes = lax.dynamic_slice_in_dim(step_sizes, x_here * z_size, z_size)[:, None, None]

    weighted = jnp.sum(step_sizes * attended.reshape(z_size, slice_tokens, -1), axis=0)
    width = weighted.shape[1]
    sides = lax.all_gather(jnp.concatenate([weighted, rows_here[0]], axis=1), "x")
    weighted = jnp.zeros_like(weighted)
    for at in range(x_size - 1):
        weighted = weighted + jnp.where(at < x_here, sides[at, :, :width], 0.0)
    high = lax.reduce_precision(weighted, 8, 7)
    terms = [high.astype(jnp.bfloat16), (weighted - high).astype(jnp.bfloat16)]
    rows = jnp.concatenate([attended, *terms])

    rows = lax.all_gather(rows, TP)
    out_rows = out_rows.reshape(rows.shape[0], width, block)
    product = jnp.einsum("jtk,jkn->tn", rows, out_rows, preferred_element_type=jnp.float32)
    velocity = product[:token_count].reshape(z_size, slice_tokens, block)
    terms = product[token_count:].reshape(2, slice_tokens, block)
    start = sides[0, :, width:] + (terms[0] + terms[1])
    drift = step_sizes * velocity

    running = drift
    reach = 1
    while reach < z_size:
        running = running + jnp.pad(running[:-reach], ((reach, 0), (0, 0), (0, 0)))
        reach *= 2
    change = start + jnp.pad(running[:-1], ((1, 0), (0, 0), (0, 0))) - rows_here
    change_sum = jnp.sum(change * change, axis=(1, 2), keepdims=True)
    change_sum = jnp.broadcast_to(change_sum, (z_size, slice_tokens, HD))
    sent = jnp.concatenate([start + running, change_sum], axis=2)
    got = lax.all_to_all(sent, "z", 0, 0)
    new_rows = got[:, :, :block].reshape(token_count, block)
    change_sum = tp_sum(jnp.sum(got[:, 0, block]))
    error_value = change_sum / (token_count * full_width)
    return (new_rows[None], error_value.reshape(1))


def solution(mesh):
    fine = Mesh(mesh.devices.reshape(4, 16, 4, 2), ("x", "z", "y", "core"))
    placed = (
        P(STEP, None, TP),
        P(),
        P(None, TP),
        P(None, TP),
        P(TP),
        P(TP),
        P(STEP, TP),
        P(STEP, TP),
    )
    return jax.shard_map(
        on_device,
        mesh=fine,
        in_specs=placed,
        out_specs=(P(STEP, None, TP), P(STEP)),
        check_vma=False,
    )
```

```python
import math

import jax
import jax.numpy as jnp
from jax import lax
from jax.sharding import Mesh
from jax.sharding import PartitionSpec as P

HD = 128
STEP = ("x", "z")
TP = ("y", "core")

epsilon = 1e-06


def sigma_of(levels):
    scaled = levels.astype(jnp.float32) / 1000.0
    return 5.0 * scaled / (1.0 + 4.0 * scaled)


def tp_sum(value):
    return lax.psum(lax.psum(value, "y"), "core")


def transpose_plane(value):
    side = lax.axis_size("x")
    pairs = [(a * side + b, b * side + a) for a in range(side) for b in range(side)]
    return lax.ppermute(value, ("x", "y"), pairs)


def on_device(trajectory, timesteps, context_keys, context_values, ln_gain, q_gain, w_query, w_out):
    latent = trajectory[0]
    token_count, block = latent.shape
    full_width = block * lax.axis_size(TP)
    x_size = lax.axis_size("x")

    z_size = lax.axis_size("z")
    x_here = lax.axis_index("x")
    slice_tokens = token_count // z_size

    depth, cols = w_query.shape
    both = jnp.concatenate([jnp.pad(w_query, ((0, 0), (0, block - cols))), w_out])
    both = lax.all_gather(both, "z")

    rows_here = lax.all_to_all(latent.reshape(z_size, slice_tokens, block), "z", 0, 0)
    latent = rows_here.reshape(token_count, block)

    sums = jnp.stack([jnp.sum(latent, axis=-1), jnp.sum(latent * latent, axis=-1)])
    sums = tp_sum(sums) / full_width
    row_mean, row_square = sums[0][:, None], sums[1][:, None]
    row_var = row_square - row_mean * row_mean
    normed = ((latent - row_mean) * lax.rsqrt(row_var + epsilon) * ln_gain).astype(jnp.bfloat16)

    flipped = transpose_plane(normed)
    gathered = lax.all_gather(flipped, "y")
    parts = [lax.all_gather(gathered[:, :, :cols], "core"), lax.all_gather(gathered[:, :, cols:], "core")]
    both, parts = lax.optimization_barrier((both, parts))
    query_weights = both[:, :depth, :cols].reshape(2, block, cols)
    out_rows = both[:, depth:].reshape(-1, block)
    out_rows = lax.all_gather(out_rows, "x", axis=0, tiled=True)
    partial = 0.0
    for part, weights in zip(parts, (query_weights[:, :cols], query_weights[:, cols:])):
        partial += jnp.einsum("cxtk,ckn->xtn", part, weights, preferred_element_type=jnp.float32)
    query = jnp.sum(lax.all_to_all(partial, "x", 0, 0), axis=0)
    query_width = query.shape[1] * lax.axis_size(TP)
    square_sum = tp_sum(jnp.sum(query * query, axis=-1))
    query_scale = lax.rsqrt(square_sum / query_width + epsilon)[:, None]
    q_normed = (query * query_scale * q_gain).astype(jnp.bfloat16)
    local_heads = query.shape[1] // HD
    q_heads = q_normed.reshape(token_count, local_heads, HD)
    key_heads = context_keys.reshape(context_keys.shape[0], local_heads, HD)
    value_heads = context_values.reshape(context_values.shape[0], local_heads, HD)
    scores = jnp.einsum(
        "thd,khd->htk", q_heads, key_heads, preferred_element_type=jnp.float32
    ) / math.sqrt(HD)
    soft_weights = jax.nn.softmax(scores, axis=-1).astype(jnp.bfloat16)
    attended = jnp.einsum(
        "htk,khd->thd", soft_weights, value_heads, preferred_element_type=jnp.float32
    )
    attended = attended.reshape(token_count, local_heads * HD).astype(jnp.bfloat16)
    attended = lax.optimization_barrier(attended)

    later = jnp.concatenate([timesteps[1:], jnp.zeros((1,), timesteps.dtype)])
    step_sizes = sigma_of(later) - sigma_of(timesteps)
    step_sizes = lax.dynamic_slice_in_dim(step_sizes, x_here * z_size, z_size)[:, None, None]

    weighted = jnp.sum(step_sizes * attended.reshape(z_size, slice_tokens, -1), axis=0)
    width = weighted.shape[1]
    sides = lax.all_gather(jnp.concatenate([weighted, rows_here[0]], axis=1), "x")
    weighted = jnp.zeros_like(weighted)
    for at in range(x_size - 1):
        weighted = weighted + jnp.where(at < x_here, sides[at, :, :width], 0.0)
    high = lax.reduce_precision(weighted, 8, 7)
    terms = [high.astype(jnp.bfloat16), (weighted - high).astype(jnp.bfloat16)]
    rows = jnp.concatenate([attended, *terms])

    rows = lax.all_gather(rows, TP)
    out_rows = out_rows.reshape(rows.shape[0], width, block)
    product = jnp.einsum("jtk,jkn->tn", rows, out_rows, preferred_element_type=jnp.float32)
    velocity = product[:token_count].reshape(z_size, slice_tokens, block)
    terms = product[token_count:].reshape(2, slice_tokens, block)
    start = sides[0, :, width:] + (terms[0] + terms[1])
    drift = step_sizes * velocity

    running = drift
    reach = 1
    while reach < z_size:
        running = running + jnp.pad(running[:-reach], ((reach, 0), (0, 0), (0, 0)))
        reach *= 2
    change = start + jnp.pad(running[:-1], ((1, 0), (0, 0), (0, 0))) - rows_here
    change_sum = jnp.sum(change * change, axis=(1, 2), keepdims=True)
    change_sum = jnp.broadcast_to(change_sum, (z_size, slice_tokens, HD))
    sent = jnp.concatenate([start + running, change_sum], axis=2)
    got = lax.all_to_all(sent, "z", 0, 0)
    new_rows = got[:, :, :block].reshape(token_count, block)
    change_sum = tp_sum(jnp.sum(got[:, 0, block]))
    error_value = change_sum / (token_count * full_width)
    return (new_rows[None], error_value.reshape(1))


def solution(mesh):
    fine = Mesh(mesh.devices.reshape(4, 16, 4, 2), ("x", "z", "y", "core"))
    placed = (
        P(STEP, None, TP),
        P(),
        P(None, TP),
        P(None, TP),
        P(TP),
        P(TP),
        P(STEP, TP),
        P(STEP, TP),
    )
    return jax.shard_map(
        on_device,
        mesh=fine,
        in_specs=placed,
        out_specs=(P(STEP, None, TP), P(STEP)),
        check_vma=False,
    )
```
